512 devices in a mesh: seq: 64 (over z, y), head: 8 (over x, core).
Axes of the slice: x: 4, y: 8, z: 8, core: 2. Of those that a mesh axis runs over, the one named last changes fastest.
Arguments:
- hidden: bfloat16 [32768, 4096], P('seq', 'head'), may hold values from -6 to 6
- queries: bfloat16 [32768, 4096], P('seq', 'head'), may hold values from -120 to 120
- keys_low: bfloat16 [32768, 1024], P('seq', 'head'), may hold values from -6 to 6
- values_low: bfloat16 [32768, 1024], P('seq', 'head'), may hold values from -6 to 6
- out_weight: bfloat16 [4096, 4096], P('head', 'seq'), may hold values from -0.09375 to 0.09375
- norm_gain: float32 [4096], replicated, may hold values from 0.25 to 1.75
- query_weight: bfloat16 [4096, 4096], P('seq', 'head'), may hold values from -3 to 3
- key_weight: bfloat16 [4096, 1024], P('seq', 'head'), may hold values from -0.09375 to 0.09375
- value_weight: bfloat16 [4096, 1024], P('seq', 'head'), may hold values from -0.09375 to 0.09375
- keep_index: int32 [64, 256], P('seq'), may hold values from 0 to 511, as said below
- keep_count: int32 [64], replicated, may hold values from 128 to 256, as said below
Outputs:
- merged_attention: bfloat16 [16384, 4096], P('seq', 'head')
The draws below stay inside these ranges and needn't reach their ends.
Inputs may be any that keep to these rules, and one draw needn't show every extreme that they name: `keep_index`: each block's valid positions are distinct, in increasing order; padded slots hold 0. `keep_count`: the first block keeps 256 positions.
All inputs are finite; a program needn't handle non-finite values.
Results may differ from the reference program's by a relative error of at most 0.04.
Values may be sent and summed in bfloat16 or wider, within the bound.
No kernel may reach another device: no remote copies, remote signals or barrier semaphores. Data moves between devices by JAX's collectives and lax.ppermute only.
A program may use at most 64 MiB of HBM per device.

```python
import jax
import jax.numpy as jnp
from jax import lax

D = 4096
HEADS = 32
KV_HEADS = 8
HD = 128
BLOCK = 512
KMAX = 256
BLOCKS_DEV = 1
BLOCKS = 64
TOKENS = 32768
N_SEQ = 64
N_HEAD = 8


def keep_tables(key):
    counts = jax.random.randint(jax.random.fold_in(key, 1), (BLOCKS,), KMAX // 2, KMAX + 1)
    counts = counts.at[0].set(KMAX)
    scores = jax.random.randint(jax.random.fold_in(key, 2), (BLOCKS, BLOCK), 0, 1 << 20)
    scores = scores * BLOCK + jnp.arange(BLOCK)[None, :]
    order = jnp.argsort(scores, axis=1, stable=True).astype(jnp.int32)
    taken = order[:, :KMAX]
    slot = jnp.arange(KMAX)[None, :]
    masked = jnp.where(slot < counts[:, None], taken, BLOCK + 7)
    ordered = jnp.sort(masked, axis=1)
    return (jnp.where(ordered < BLOCK, ordered, 0).astype(jnp.int32), counts.astype(jnp.int32))


def key_base(key):
    raw = jax.random.normal(jax.random.fold_in(key, 3), (TOKENS, KV_HEADS * HD), jnp.float32)
    return jnp.clip(raw, -6.0, 6.0)


def key_weight_base(key):
    raw = jax.random.normal(jax.random.fold_in(key, 5), (D, KV_HEADS * HD), jnp.float32)
    return jnp.clip(raw, -6.0, 6.0) * D ** (-0.5)


def draw_keep_index(key, part):
    return keep_tables(key)[0]


def draw_keep_count(key, part):
    return keep_tables(key)[1]


def draw_keys_low(key, part):
    return key_base(key).astype(jnp.bfloat16)


def draw_key_weight(key, part):
    return key_weight_base(key).astype(jnp.bfloat16)


def draw_query_weight(key, part):
    key = jax.random.fold_in(key, 21)
    noise = jnp.clip(jax.random.normal(key, (D, HEADS * HD), jnp.float32), -6.0, 6.0) * D ** (-0.5)
    return noise.astype(jnp.bfloat16)


def draw_queries(key, part):
    key = jax.random.fold_in(key, 11)
    noise = jnp.clip(jax.random.normal(key, (TOKENS, HEADS * HD), jnp.float32), -6.0, 6.0)
    return noise.astype(jnp.bfloat16)


def block_scale(rng, dims, pieces, least, largest):
    factor_of, own = 1.0, jax.random.fold_in(rng, 6)
    for dim, shards_of in pieces:
        steps = jnp.exp(jax.random.uniform(jax.random.fold_in(own, dim), (shards_of,), jnp.float32, least / len(pieces), largest / len(pieces)))
        factor_of = factor_of * jnp.repeat(steps, dims[dim] // shards_of).reshape([-1 if axis == dim else 1 for axis in range(len(dims))])
    return factor_of


def scatter_about(stream_key, extent, spread, limit, shards=(), held_as=jnp.bfloat16):
    entries = spread * jax.random.normal(stream_key, extent, jnp.float32)
    if shards:
        entries = entries * block_scale(stream_key, extent, shards, -0.22, 0.18)
    return jnp.clip(entries, -limit, limit).astype(held_as)


def setup_inputs(seed: int = 0) -> dict:
    splits = jax.random.split(jax.random.key(seed), 12)
    hidden = scatter_about(splits[0], (TOKENS, D), 1.0, 6.0, ((0, 64), (1, 8)))
    queries = draw_queries(jax.random.fold_in(splits[11], 71), 0)
    keys_low = draw_keys_low(jax.random.fold_in(splits[11], 71), 0)
    values_low = scatter_about(splits[3], (TOKENS, KV_HEADS * HD), 1.0, 6.0, ((0, 64), (1, 8)))
    out_weight = scatter_about(splits[4], (HEADS * HD, D), (HEADS * HD) ** -0.5, 0.09375, ((0, 8), (1, 64)))
    norm_gain = jnp.clip(1.0 + 0.15 * jax.random.normal(splits[5], (D,), jnp.float32), 0.25, 1.75)
    query_weight = draw_query_weight(jax.random.fold_in(splits[11], 71), 0)
    key_weight = draw_key_weight(jax.random.fold_in(splits[11], 71), 0)
    value_weight = scatter_about(splits[8], (D, KV_HEADS * HD), D ** -0.5, 0.09375, ((0, 64), (1, 8)))
    keep_index = draw_keep_index(jax.random.fold_in(splits[11], 71), 0)
    keep_count = draw_keep_count(jax.random.fold_in(splits[11], 71), 0)
    return {"hidden": hidden, "queries": queries, "keys_low": keys_low, "values_low": values_low, "out_weight": out_weight, "norm_gain": norm_gain, "query_weight": query_weight, "key_weight": key_weight, "value_weight": value_weight, "keep_index": keep_index, "keep_count": keep_count}


def lower_block(query_blk, key_blk, value_blk):
    group = HEADS // KV_HEADS
    query_f = query_blk.astype(jnp.float32).reshape(BLOCK, KV_HEADS, group, HD)
    key_f = key_blk.astype(jnp.float32).reshape(BLOCK, KV_HEADS, HD)
    value_f = value_blk.astype(jnp.float32).reshape(BLOCK, KV_HEADS, HD)
    scores = jnp.einsum('qhgd,khd->hgqk', query_f, key_f) / HD ** 0.5
    position = jnp.arange(BLOCK)
    causal = position[:, None] >= position[None, :]
    scores = jnp.where(causal, scores, -1e+30)
    weights = jax.nn.softmax(scores, axis=-1).astype(jnp.bfloat16)
    output = jnp.einsum('hgqk,khd->qhgd', weights.astype(jnp.float32), value_f)
    return output.astype(jnp.bfloat16).reshape(BLOCK, HEADS * HD)

def reference(hidden, queries, keys_low, values_low, out_weight, norm_gain, query_weight, key_weight, value_weight, keep_index, keep_count):
    width = HEADS * HD // N_HEAD
    weight_groups = out_weight.astype(jnp.float32).reshape(N_HEAD, width, D)

    def encode(inputs):
        query_blk, key_blk, value_blk, hidden_blk, keep_row = inputs
        attention = lower_block(query_blk, key_blk, value_blk)
        picked = attention[keep_row].astype(jnp.float32).reshape(KMAX, N_HEAD, width)
        partial_terms = jnp.einsum('rgf,gfd->grd', picked, weight_groups).astype(jnp.bfloat16)
        partial_terms = lax.optimization_barrier(partial_terms).astype(jnp.float32)
        summed = lax.optimization_barrier(jnp.sum(partial_terms, axis=0))
        state = (hidden_blk[keep_row].astype(jnp.float32) + summed).astype(jnp.bfloat16)
        state_f = state.astype(jnp.float32)
        meansq = lax.optimization_barrier(jnp.mean(state_f * state_f, axis=-1, keepdims=True))
        normed = (state_f * lax.rsqrt(meansq + 1e-05) * norm_gain[None, :]).astype(jnp.bfloat16)
        upper_q = jnp.dot(normed, query_weight, preferred_element_type=jnp.float32).astype(jnp.bfloat16)
        upper_k = jnp.dot(normed, key_weight, preferred_element_type=jnp.float32).astype(jnp.bfloat16)
        upper_v = jnp.dot(normed, value_weight, preferred_element_type=jnp.float32).astype(jnp.bfloat16)
        return (upper_q, upper_k, upper_v)
    upper_q, upper_k, upper_v = lax.map(encode, (queries.reshape(BLOCKS, BLOCK, HEADS * HD), keys_low.reshape(BLOCKS, BLOCK, KV_HEADS * HD), values_low.reshape(BLOCKS, BLOCK, KV_HEADS * HD), hidden.reshape(BLOCKS, BLOCK, D), keep_index))
    pairs = N_SEQ // 2 * BLOCKS_DEV

    def to_pairs(array):
        shaped = array.reshape((N_SEQ // 2, 2, BLOCKS_DEV) + array.shape[1:])
        return jnp.swapaxes(shaped, 1, 2).reshape((pairs, 2) + array.shape[1:])
    group = HEADS // KV_HEADS

    def merged_pair(inputs):
        pair_q, pair_k, pair_v, pair_count = inputs
        query_f = pair_q.astype(jnp.float32).reshape(2 * KMAX, KV_HEADS, group, HD)
        key_f = pair_k.astype(jnp.float32).reshape(2 * KMAX, KV_HEADS, HD)
        value_f = pair_v.astype(jnp.float32).reshape(2 * KMAX, KV_HEADS, HD)
        position = jnp.arange(2 * KMAX)
        side = position // KMAX
        local = position % KMAX
        valid = local < pair_count[side]
        same_side = (side[None, :] == side[:, None]) & (local[None, :] <= local[:, None])
        allowed = valid[None, :] & ((side[None, :] < side[:, None]) | same_side)
        scores = jnp.einsum('qhgd,khd->hgqk', query_f, key_f) / HD ** 0.5
        scores = jnp.where(allowed, scores, -1e+30)
        weights = jax.nn.softmax(scores, axis=-1).astype(jnp.bfloat16)
        output = jnp.einsum('hgqk,khd->qhgd', weights.astype(jnp.float32), value_f).reshape(2 * KMAX, HEADS * HD)
        output = jnp.where(valid[:, None], output, 0.0)
        return output.astype(jnp.bfloat16).reshape(2, KMAX, HEADS * HD)
    merged = lax.map(merged_pair, (to_pairs(upper_q), to_pairs(upper_k), to_pairs(upper_v), to_pairs(keep_count)))
    merged = merged.reshape(N_SEQ // 2, BLOCKS_DEV, 2, KMAX, HEADS * HD)
    merged = jnp.swapaxes(merged, 1, 2)
    return merged.reshape(BLOCKS * KMAX, HEADS * HD)
```

```python
import functools

import jax
import jax.numpy as jnp
from jax import lax
from jax.experimental import pallas as pl
from jax.experimental.pallas import tpu as pltpu
from jax.sharding import PartitionSpec as P

D = 4096
HEADS = 32
KV_HEADS = 8
HD = 128
BLOCK = 512
KMAX = 256
GROUP = HEADS // KV_HEADS
N_Z = 8
N_Y = 8
N_X = 4
STRIP = D // (N_Z * N_Y)
HALF = N_Y // 2 * STRIP
QW = GROUP * HD
KVW = 2 * HD
QKV = QW + KVW
LOG2E = 1.4426950408889634
SCALE = HD**-0.5 * LOG2E
NEG = -1e30
VMEM_LIMIT = 48 * 1024 * 1024

PARITY_GROUPS = [[z * N_Y + 2 * p + q for z in range(N_Z) for p in range(N_Y // 2)] for q in range(2)]
X_GROUPS = [[2 * x + c for x in range(N_X)] for c in range(2)]
CORE_SWAP = [(i, i ^ 1) for i in range(2 * N_X)]
SIBLING_SWAP = [(i, i ^ 1) for i in range(N_Z * N_Y)]
Z_HEAD_SWAP = [
    ((z * N_Y + y) * 8 + h, (h * N_Y + y) * 8 + z)
    for z in range(N_Z)
    for y in range(N_Y)
    for h in range(8)
]


def params():
    return pltpu.CompilerParams(vmem_limit_bytes=VMEM_LIMIT)


def dot(a, b):
    return jnp.dot(a, b, preferred_element_type=jnp.float32)


def dot_t(a, b):
    return lax.dot_general(a, b, (((1,), (1,)), ((), ())), preferred_element_type=jnp.float32)


def attend(scores, values):
    top = jnp.max(scores, axis=1, keepdims=True)
    unnormed = jnp.exp2(scores - top)
    total = jnp.sum(unnormed, axis=1, keepdims=True)
    return dot(unnormed.astype(jnp.bfloat16), values) / total


def lower_kernel(index_ref, q_ref, k_ref, v_ref, hidden_ref, out_ref):
    index = index_ref[...]
    column = lax.broadcasted_iota(jnp.int32, (KMAX, BLOCK), 1)
    pick = (column == index).astype(jnp.bfloat16)
    causal = column <= index
    queries = dot(pick, q_ref[...]).astype(jnp.bfloat16)
    keys = k_ref[...]
    values = v_ref[...]
    for g in range(GROUP):
        cols = slice(g * HD, (g + 1) * HD)
        scores = jnp.where(causal, dot_t(queries[:, cols], keys) * SCALE, NEG)
        out_ref[:, cols] = attend(scores, values).astype(jnp.bfloat16)
    out_ref[:, QW:] = dot(pick, hidden_ref[...]).astype(jnp.bfloat16)


def lower(index, queries, keys, values, hidden):
    return pl.pallas_call(
        lower_kernel,
        out_shape=jax.ShapeDtypeStruct((KMAX, 2 * QW), jnp.bfloat16),
        compiler_params=params(),
        name="lower",
    )(index, queries, keys, values, hidden)


def project_kernel(place_ref, mine_ref, other_ref, weight_ref, hid_ref, hid_pair_ref, out_ref, acc_ref):
    step = pl.program_id(0)
    core = place_ref[0]
    parity = place_ref[1]

    @pl.when(step == 0)
    def _():
        row = lax.broadcasted_iota(jnp.int32, (QW, HALF), 0)
        col = lax.broadcasted_iota(jnp.int32, (QW, HALF), 1)
        source = (col // STRIP) * (2 * STRIP) + parity * STRIP + col % STRIP
        pick = (row == source).astype(jnp.bfloat16)
        acc_ref[:KMAX] = dot(hid_ref[...], pick)
        acc_ref[KMAX:] = dot(hid_pair_ref[...], pick)

    def share(core_of):
        return weight_ref[pl.ds(core_of * 4, 4)].reshape(HALF, QW)

    acc_ref[...] += dot_t(mine_ref[0], share(core)) + dot_t(other_ref[0], share(1 - core))

    @pl.when(step == N_X - 1)
    def _():
        state = acc_ref[...].astype(jnp.bfloat16)
        for x in range(N_X):
            out_ref[x] = state


def project(place, mine, other, weights, hid, hid_pair):
    rows = 2 * KMAX
    return pl.pallas_call(
        project_kernel,
        grid=(N_X,),
        in_specs=[
            pl.BlockSpec(memory_space=pltpu.SMEM),
            pl.BlockSpec((1, rows, QW), lambda i: (i, 0, 0)),
            pl.BlockSpec((1, rows, QW), lambda i: (i, 0, 0)),
            pl.BlockSpec((8, STRIP, QW), lambda i: (i, 0, 0)),
            pl.BlockSpec((KMAX, QW), lambda i: (0, 1)),
            pl.BlockSpec((KMAX, QW), lambda i: (0, 1)),
        ],
        out_specs=pl.BlockSpec((N_X, rows, HALF), lambda i: (0, 0, 0)),
        out_shape=jax.ShapeDtypeStruct((N_X, rows, HALF), jnp.bfloat16),
        scratch_shapes=[pltpu.VMEM((rows, HALF), jnp.float32)],
        compiler_params=params(),
        name="project",
    )(place, mine, other, weights, hid, hid_pair)


def qkv_kernel(
    place_ref, mine_ref, other_ref, wq_ref, wkv_ref, gain_ref, own_ref, pair_kv_ref, square_ref, send_ref, acc_ref, sq_ref
):
    step = pl.program_id(0)
    core = place_ref[0]

    @pl.when(step == 0)
    def _():
        acc_ref[...] = jnp.zeros_like(acc_ref)
        sq_ref[...] = jnp.zeros_like(sq_ref)

    def add(part_ref, core_of):
        state = part_ref[0].astype(jnp.float32)
        squares = state * state
        sq_ref[...] += squares[:, :HD] + squares[:, HD:]
        scaled = (state * gain_ref[2 * step + core_of]).astype(jnp.bfloat16)
        wq = wq_ref[pl.ds(core_of * 4, 4)].reshape(HALF, QW)
        packed = wkv_ref[pl.ds(core_of * 4, 4)]
        wkv = jnp.concatenate([packed[:, :, :KVW], packed[:, :, KVW:]], axis=1).reshape(HALF, KVW)
        acc_ref[:, :QW] += dot(scaled, wq)
        acc_ref[:, QW:] += dot(scaled, wkv)

    add(mine_ref, core)
    add(other_ref, 1 - core)

    @pl.when(step == N_X - 1)
    def _():
        total = jnp.sum(sq_ref[...], axis=1, keepdims=True)
        own_ref[...] = acc_ref[:KMAX]
        pair_kv_ref[...] = acc_ref[KMAX:, QW:]
        square_ref[...] = jnp.broadcast_to(total, square_ref.shape)
        send_ref[:, :QKV] = acc_ref[KMAX:].astype(jnp.bfloat16)
        send_ref[:, QKV : QKV + KVW] = acc_ref[:KMAX, QW:].astype(jnp.bfloat16)
        high = total.astype(jnp.bfloat16).astype(jnp.float32)
        low = total - high
        lane = lax.broadcasted_iota(jnp.int32, (KMAX, HD), 1)
        tail = jnp.where(
            lane == 0,
            high[KMAX:],
            jnp.where(lane == 1, low[KMAX:], jnp.where(lane == 2, high[:KMAX], low[:KMAX])),
        )
        send_ref[:, QKV + KVW :] = tail.astype(jnp.bfloat16)


def qkv(place, mine, other, weights, gain):
    rows = 2 * KMAX
    sent = QKV + KVW + HD
    return pl.pallas_call(
        qkv_kernel,
        grid=(N_X,),
        in_specs=[
            pl.BlockSpec(memory_space=pltpu.SMEM),
            pl.BlockSpec((1, rows, HALF), lambda i: (i, 0, 0)),
            pl.BlockSpec((1, rows, HALF), lambda i: (i, 0, 0)),
            pl.BlockSpec((8, STRIP, QW), lambda i: (i, 1, 0)),
            pl.BlockSpec((8, STRIP // 2, QW), lambda i: (i, 4, 0)),
            pl.BlockSpec((8, 1, HALF), lambda i: (0, 0, 0)),
        ],
        out_specs=[
            pl.BlockSpec((KMAX, QKV), lambda i: (0, 0)),
            pl.BlockSpec((KMAX, KVW), lambda i: (0, 0)),
            pl.BlockSpec((rows, HD), lambda i: (0, 0)),
            pl.BlockSpec((KMAX, sent), lambda i: (0, 0)),
        ],
        out_shape=[
            jax.ShapeDtypeStruct((KMAX, QKV), jnp.float32),
            jax.ShapeDtypeStruct((KMAX, KVW), jnp.float32),
            jax.ShapeDtypeStruct((rows, HD), jnp.float32),
            jax.ShapeDtypeStruct((KMAX, sent), jnp.bfloat16),
        ],
        scratch_shapes=[
            pltpu.VMEM((rows, QKV), jnp.float32),
            pltpu.VMEM((rows, HD), jnp.float32),
        ],
        compiler_params=params(),
        name="qkv",
    )(place, mine, other, weights, weights, gain)


def upper_kernel(place_ref, own_ref, pair_kv_ref, square_ref, got_ref, out_ref):
    parity = place_ref[1]
    own_count = place_ref[2]
    left_count = place_ref[3]
    tail = got_ref[:, QKV + KVW :].astype(jnp.float32)
    own_sum = square_ref[:KMAX, :1] + (tail[:, 0:1] + tail[:, 1:2])
    pair_sum = square_ref[KMAX:, :1] + (tail[:, 2:3] + tail[:, 3:4])
    own_inv = lax.rsqrt(own_sum / D + 1e-05)
    pair_inv = lax.rsqrt(pair_sum / D + 1e-05)
    own = ((own_ref[...] + got_ref[:, :QKV].astype(jnp.float32)) * own_inv).astype(jnp.bfloat16)
    pair = (pair_kv_ref[...] + got_ref[:, QKV : QKV + KVW].astype(jnp.float32)) * pair_inv
    pair = pair.astype(jnp.bfloat16)
    keys = jnp.concatenate([pair[:, :HD], own[:, QW : QW + HD]], axis=0)
    values = jnp.concatenate([pair[:, HD:], own[:, QW + HD :]], axis=0)
    row = lax.broadcasted_iota(jnp.int32, (KMAX, 2 * KMAX), 0)
    col = lax.broadcasted_iota(jnp.int32, (KMAX, 2 * KMAX), 1)
    from_left = col < left_count * parity
    from_own = (col >= KMAX) & (col - KMAX <= row) & (col - KMAX < own_count)
    allowed = from_left | from_own
    valid = lax.broadcasted_iota(jnp.int32, (KMAX, HD), 0) < own_count
    for g in range(GROUP):
        cols = slice(g * HD, (g + 1) * HD)
        scores = jnp.where(allowed, dot_t(own[:, cols], keys) * SCALE, NEG)
        out_ref[:, cols] = jnp.where(valid, attend(scores, values), 0.0).astype(jnp.bfloat16)


def upper(place, own, pair_kv, squares, got):
    return pl.pallas_call(
        upper_kernel,
        in_specs=[pl.BlockSpec(memory_space=pltpu.SMEM)] + [pl.BlockSpec(memory_space=pltpu.VMEM)] * 4,
        out_shape=jax.ShapeDtypeStruct((KMAX, QW), jnp.bfloat16),
        compiler_params=params(),
        name="upper",
    )(place, own, pair_kv, squares, got)


def gather_head(x):
    mine = lax.all_to_all(x, "head", 0, 0, axis_index_groups=X_GROUPS, tiled=True)
    return mine, lax.ppermute(mine, "head", CORE_SWAP)


def per_device(
    hidden,
    queries,
    keys_low,
    values_low,
    out_weight,
    norm_gain,
    query_weight,
    key_weight,
    value_weight,
    keep_index,
    keep_count,
):
    seq = lax.axis_index("seq")
    parity = seq % 2
    core = lax.axis_index("head") % 2
    own_count = lax.dynamic_index_in_dim(keep_count, seq, keepdims=False)
    left_count = lax.dynamic_index_in_dim(keep_count, jnp.maximum(seq - 1, 0), keepdims=False)
    place = jnp.stack([core, parity, own_count, left_count]).astype(jnp.int32)

    columns = lax.ppermute(out_weight.T, ("seq", "head"), Z_HEAD_SWAP)
    kv = jnp.concatenate([key_weight, value_weight], axis=1)
    kv = jnp.concatenate([kv[: STRIP // 2], kv[STRIP // 2 :]], axis=1)
    packed = jnp.concatenate([columns, query_weight, kv], axis=0)
    weights = lax.all_gather(packed, "seq", axis=0, axis_index_groups=PARITY_GROUPS)

    kept = lower(keep_index.reshape(KMAX, 1), queries, keys_low, values_low, hidden)
    kept_pair = lax.ppermute(kept, "seq", SIBLING_SWAP)
    attention = jnp.concatenate([kept[:, :QW], kept_pair[:, :QW]], axis=0)
    mine, other = gather_head(jnp.broadcast_to(attention[None], (N_X,) + attention.shape))

    state = project(place, mine, other, weights, kept, kept_pair)
    mine, other = gather_head(state)
    gain = lax.dynamic_index_in_dim(
        norm_gain.reshape(8, N_Y // 2, 2, STRIP), parity, axis=2, keepdims=False
    ).reshape(8, 1, HALF)
    own, pair_kv, squares, send = qkv(place, mine, other, weights, gain)
    got = lax.ppermute(send, "seq", SIBLING_SWAP)
    return upper(place, own, pair_kv, squares, got)


def solution(mesh):
    in_specs = (
        P("seq", "head"),
        P("seq", "head"),
        P("seq", "head"),
        P("seq", "head"),
        P("head", "seq"),
        P(),
        P("seq", "head"),
        P("seq", "head"),
        P("seq", "head"),
        P("seq", None),
        P(),
    )
    out_specs = P("seq", "head")
    return jax.shard_map(
        per_device, mesh=mesh, in_specs=in_specs, out_specs=out_specs, check_vma=False
    )
```

```python
import functools

import jax
import jax.numpy as jnp
from jax import lax
from jax.experimental import pallas as pl
from jax.experimental.pallas import tpu as pltpu
from jax.sharding import PartitionSpec as P

D = 4096
HEADS = 32
KV_HEADS = 8
HD = 128
BLOCK = 512
KMAX = 256
GROUP = HEADS // KV_HEADS
N_Z = 8
N_Y = 8
N_X = 4
STRIP = D // (N_Z * N_Y)
HALF = N_Y // 2 * STRIP
QW = GROUP * HD
KVW = 2 * HD
QKV = QW + KVW
LOG2E = 1.4426950408889634
SCALE = HD**-0.5 * LOG2E
NEG = -1e30
VMEM_LIMIT = 48 * 1024 * 1024

Z_GROUPS = [[z * N_Y + y for z in range(N_Z)] for y in range(N_Y)]
X_GROUPS = [[2 * x + c for x in range(N_X)] for c in range(2)]
CORE_SWAP = [(i, i ^ 1) for i in range(2 * N_X)]
SIBLING_SWAP = [(i, i ^ 1) for i in range(N_Z * N_Y)]
PARITY_GROUPS = [[z * N_Y + 2 * p + q for p in range(N_Y // 2)] for z in range(N_Z) for q in range(2)]


def params():
    return pltpu.CompilerParams(vmem_limit_bytes=VMEM_LIMIT)


def dot(a, b):
    return jnp.dot(a, b, preferred_element_type=jnp.float32)


def dot_t(a, b):
    return lax.dot_general(a, b, (((1,), (1,)), ((), ())), preferred_element_type=jnp.float32)


def attend(scores, values):
    top = jnp.max(scores, axis=1, keepdims=True)
    unnormed = jnp.exp2(scores - top)
    total = jnp.sum(unnormed, axis=1, keepdims=True)
    return dot(unnormed.astype(jnp.bfloat16), values) / total


def lower_kernel(index_ref, q_ref, k_ref, v_ref, hidden_ref, out_ref):
    index = index_ref[...]
    column = lax.broadcasted_iota(jnp.int32, (KMAX, BLOCK), 1)
    pick = (column == index).astype(jnp.bfloat16)
    causal = column <= index
    queries = dot(pick, q_ref[...]).astype(jnp.bfloat16)
    keys = k_ref[...]
    values = v_ref[...]
    for g in range(GROUP):
        cols = slice(g * HD, (g + 1) * HD)
        scores = jnp.where(causal, dot_t(queries[:, cols], keys) * SCALE, NEG)
        out_ref[:, cols] = attend(scores, values).astype(jnp.bfloat16)
    out_ref[:, QW:] = dot(pick, hidden_ref[...]).astype(jnp.bfloat16)


def lower(index, queries, keys, values, hidden):
    return pl.pallas_call(
        lower_kernel,
        out_shape=jax.ShapeDtypeStruct((KMAX, 2 * QW), jnp.bfloat16),
        compiler_params=params(),
        name="lower",
    )(index, queries, keys, values, hidden)


def project_kernel(place_ref, own_ref, pair_ref, weight_ref, keep_ref, send_ref):
    core = place_ref[0]
    mine = weight_ref[core]
    other = weight_ref[1 - core]
    keep_ref[0, :KMAX] = dot_t(own_ref[...], mine)
    keep_ref[0, KMAX:] = dot_t(pair_ref[...], mine)
    send_ref[0, :KMAX] = dot_t(own_ref[...], other).astype(jnp.bfloat16)
    send_ref[0, KMAX:] = dot_t(pair_ref[...], other).astype(jnp.bfloat16)


def project(place, kept, kept_pair, weights):
    shape = (N_X, 2 * KMAX, HALF)
    block = pl.BlockSpec((1, 2 * KMAX, HALF), lambda i: (i, 0, 0))
    return pl.pallas_call(
        project_kernel,
        grid=(N_X,),
        in_specs=[
            pl.BlockSpec(memory_space=pltpu.SMEM),
            pl.BlockSpec((KMAX, QW), lambda i: (0, 0)),
            pl.BlockSpec((KMAX, QW), lambda i: (0, 0)),
            pl.BlockSpec((2, HALF, QW), lambda i: (i, 0, 0)),
        ],
        out_specs=[block, block],
        out_shape=[
            jax.ShapeDtypeStruct(shape, jnp.float32),
            jax.ShapeDtypeStruct(shape, jnp.bfloat16),
        ],
        compiler_params=params(),
        name="project",
    )(place, kept, kept_pair, weights)


def state_kernel(place_ref, parts_ref, hid_ref, hid_pair_ref, out_ref):
    parity = place_ref[1]
    row = lax.broadcasted_iota(jnp.int32, (QW, HALF), 0)
    col = lax.broadcasted_iota(jnp.int32, (QW, HALF), 1)
    source = (col // STRIP) * (2 * STRIP) + parity * STRIP + col % STRIP
    pick = (row == source).astype(jnp.bfloat16)
    for half, hid in enumerate((hid_ref, hid_pair_ref)):
        rows = slice(half * KMAX, (half + 1) * KMAX)
        total = dot(hid[...], pick)
        for x in range(N_X):
            total += parts_ref[x, rows].astype(jnp.float32)
        state = total.astype(jnp.bfloat16)
        for x in range(N_X):
            out_ref[x, rows] = state


def add_up(place, parts, kept, kept_pair):
    shape = (N_X, 2 * KMAX, HALF)
    return pl.pallas_call(
        state_kernel,
        grid=(1,),
        in_specs=[
            pl.BlockSpec(memory_space=pltpu.SMEM),
            pl.BlockSpec(shape, lambda i: (0, 0, 0)),
            pl.BlockSpec((KMAX, QW), lambda i: (0, 1)),
            pl.BlockSpec((KMAX, QW), lambda i: (0, 1)),
        ],
        out_specs=pl.BlockSpec(shape, lambda i: (0, 0, 0)),
        out_shape=jax.ShapeDtypeStruct(shape, jnp.bfloat16),
        compiler_params=params(),
        name="state",
    )(place, parts, kept, kept_pair)


def qkv_kernel(
    place_ref, mine_ref, other_ref, wq_ref, wkv_ref, gain_ref, own_ref, pair_kv_ref, square_ref, send_ref, acc_ref, sq_ref
):
    step = pl.program_id(0)
    core = place_ref[0]

    @pl.when(step == 0)
    def _():
        acc_ref[...] = jnp.zeros_like(acc_ref)
        sq_ref[...] = jnp.zeros_like(sq_ref)

    def add(part_ref, core_of):
        state = part_ref[0].astype(jnp.float32)
        squares = state * state
        sq_ref[...] += squares[:, :HD] + squares[:, HD:]
        scaled = (state * gain_ref[2 * step + core_of]).astype(jnp.bfloat16)
        wq = wq_ref[pl.ds(core_of * 4, 4)].reshape(HALF, QW)
        packed = wkv_ref[pl.ds(core_of * 4, 4)]
        wkv = jnp.concatenate([packed[:, :, :KVW], packed[:, :, KVW:]], axis=1).reshape(HALF, KVW)
        acc_ref[:, :QW] += dot(scaled, wq)
        acc_ref[:, QW:] += dot(scaled, wkv)

    add(mine_ref, core)
    add(other_ref, 1 - core)

    @pl.when(step == N_X - 1)
    def _():
        total = jnp.sum(sq_ref[...], axis=1, keepdims=True)
        own_ref[...] = acc_ref[:KMAX]
        pair_kv_ref[...] = acc_ref[KMAX:, QW:]
        square_ref[...] = jnp.broadcast_to(total, square_ref.shape)
        send_ref[:, :QKV] = acc_ref[KMAX:].astype(jnp.bfloat16)
        send_ref[:, QKV : QKV + KVW] = acc_ref[:KMAX, QW:].astype(jnp.bfloat16)
        high = total.astype(jnp.bfloat16).astype(jnp.float32)
        low = total - high
        lane = lax.broadcasted_iota(jnp.int32, (KMAX, HD), 1)
        tail = jnp.where(
            lane == 0,
            high[KMAX:],
            jnp.where(lane == 1, low[KMAX:], jnp.where(lane == 2, high[:KMAX], low[:KMAX])),
        )
        send_ref[:, QKV + KVW :] = tail.astype(jnp.bfloat16)


def qkv(place, mine, other, weights, gain):
    rows = 2 * KMAX
    sent = QKV + KVW + HD
    return pl.pallas_call(
        qkv_kernel,
        grid=(N_X,),
        in_specs=[
            pl.BlockSpec(memory_space=pltpu.SMEM),
            pl.BlockSpec((1, rows, HALF), lambda i: (i, 0, 0)),
            pl.BlockSpec((1, rows, HALF), lambda i: (i, 0, 0)),
            pl.BlockSpec((8, STRIP, QW), lambda i: (i, 0, 0)),
            pl.BlockSpec((8, STRIP // 2, QW), lambda i: (i, 2, 0)),
            pl.BlockSpec((8, 1, HALF), lambda i: (0, 0, 0)),
        ],
        out_specs=[
            pl.BlockSpec((KMAX, QKV), lambda i: (0, 0)),
            pl.BlockSpec((KMAX, KVW), lambda i: (0, 0)),
            pl.BlockSpec((rows, HD), lambda i: (0, 0)),
            pl.BlockSpec((KMAX, sent), lambda i: (0, 0)),
        ],
        out_shape=[
            jax.ShapeDtypeStruct((KMAX, QKV), jnp.float32),
            jax.ShapeDtypeStruct((KMAX, KVW), jnp.float32),
            jax.ShapeDtypeStruct((rows, HD), jnp.float32),
            jax.ShapeDtypeStruct((KMAX, sent), jnp.bfloat16),
        ],
        scratch_shapes=[
            pltpu.VMEM((rows, QKV), jnp.float32),
            pltpu.VMEM((rows, HD), jnp.float32),
        ],
        compiler_params=params(),
        name="qkv",
    )(place, mine, other, weights, weights, gain)


def upper_kernel(place_ref, own_ref, pair_kv_ref, square_ref, got_ref, out_ref):
    parity = place_ref[1]
    own_count = place_ref[2]
    left_count = place_ref[3]
    tail = got_ref[:, QKV + KVW :].astype(jnp.float32)
    own_sum = square_ref[:KMAX, :1] + (tail[:, 0:1] + tail[:, 1:2])
    pair_sum = square_ref[KMAX:, :1] + (tail[:, 2:3] + tail[:, 3:4])
    own_inv = lax.rsqrt(own_sum / D + 1e-05)
    pair_inv = lax.rsqrt(pair_sum / D + 1e-05)
    own = ((own_ref[...] + got_ref[:, :QKV].astype(jnp.float32)) * own_inv).astype(jnp.bfloat16)
    pair = (pair_kv_ref[...] + got_ref[:, QKV : QKV + KVW].astype(jnp.float32)) * pair_inv
    pair = pair.astype(jnp.bfloat16)
    keys = jnp.concatenate([pair[:, :HD], own[:, QW : QW + HD]], axis=0)
    values = jnp.concatenate([pair[:, HD:], own[:, QW + HD :]], axis=0)
    row = lax.broadcasted_iota(jnp.int32, (KMAX, 2 * KMAX), 0)
    col = lax.broadcasted_iota(jnp.int32, (KMAX, 2 * KMAX), 1)
    from_left = col < left_count * parity
    from_own = (col >= KMAX) & (col - KMAX <= row) & (col - KMAX < own_count)
    allowed = from_left | from_own
    valid = lax.broadcasted_iota(jnp.int32, (KMAX, HD), 0) < own_count
    for g in range(GROUP):
        cols = slice(g * HD, (g + 1) * HD)
        scores = jnp.where(allowed, dot_t(own[:, cols], keys) * SCALE, NEG)
        out_ref[:, cols] = jnp.where(valid, attend(scores, values), 0.0).astype(jnp.bfloat16)


def upper(place, own, pair_kv, squares, got):
    return pl.pallas_call(
        upper_kernel,
        in_specs=[pl.BlockSpec(memory_space=pltpu.SMEM)] + [pl.BlockSpec(memory_space=pltpu.VMEM)] * 4,
        out_shape=jax.ShapeDtypeStruct((KMAX, QW), jnp.bfloat16),
        compiler_params=params(),
        name="upper",
    )(place, own, pair_kv, squares, got)


def gather_head(x):
    mine = lax.all_to_all(x, "head", 0, 0, axis_index_groups=X_GROUPS, tiled=True)
    return mine, lax.ppermute(mine, "head", CORE_SWAP)


def gather_seq(shard):
    some = lax.all_gather(shard, "seq", axis=0, axis_index_groups=PARITY_GROUPS, tiled=True)
    return lax.all_gather(some, "seq", axis=0, axis_index_groups=Z_GROUPS)


def per_device(
    hidden,
    queries,
    keys_low,
    values_low,
    out_weight,
    norm_gain,
    query_weight,
    key_weight,
    value_weight,
    keep_index,
    keep_count,
):
    seq = lax.axis_index("seq")
    parity = seq % 2
    core = lax.axis_index("head") % 2
    own_count = lax.dynamic_index_in_dim(keep_count, seq, keepdims=False)
    left_count = lax.dynamic_index_in_dim(keep_count, jnp.maximum(seq - 1, 0), keepdims=False)
    place = jnp.stack([core, parity, own_count, left_count]).astype(jnp.int32)

    out_weights = gather_seq(out_weight.T)

    kept = lower(keep_index.reshape(KMAX, 1), queries, keys_low, values_low, hidden)
    kept_pair = lax.ppermute(kept, "seq", SIBLING_SWAP)

    kv = jnp.concatenate([key_weight, value_weight], axis=1)
    kv = jnp.concatenate([kv[: STRIP // 2], kv[STRIP // 2 :]], axis=1)
    qkv_weights = gather_seq(jnp.concatenate([query_weight, kv], axis=0))
    qkv_weights = qkv_weights.reshape(N_Z * N_Y // 2, STRIP + STRIP // 2, QW)

    keep, send = project(place, kept, kept_pair, out_weights)
    got = lax.ppermute(send, "head", CORE_SWAP)
    parts = (keep + got.astype(jnp.float32)).astype(jnp.bfloat16)
    parts = lax.all_to_all(parts, "head", 0, 0, axis_index_groups=X_GROUPS, tiled=True)
    mine, other = gather_head(add_up(place, parts, kept, kept_pair))

    gain = lax.dynamic_index_in_dim(
        norm_gain.reshape(8, N_Y // 2, 2, STRIP), parity, axis=2, keepdims=False
    ).reshape(8, 1, HALF)
    own, pair_kv, squares, send = qkv(place, mine, other, qkv_weights, gain)
    got = lax.ppermute(send, "seq", SIBLING_SWAP)
    return upper(place, own, pair_kv, squares, got)


def solution(mesh):
    in_specs = (
        P("seq", "head"),
        P("seq", "head"),
        P("seq", "head"),
        P("seq", "head"),
        P("head", "seq"),
        P(),
        P("seq", "head"),
        P("seq", "head"),
        P("seq", "head"),
        P("seq", None),
        P(),
    )
    out_specs = P("seq", "head")
    return jax.shard_map(
        per_device, mesh=mesh, in_specs=in_specs, out_specs=out_specs, check_vma=False
    )
```

```python
import functools

import jax
import jax.numpy as jnp
from jax import lax
from jax.experimental import pallas as pl
from jax.experimental.pallas import tpu as pltpu
from jax.sharding import PartitionSpec as P

D = 4096
HEADS = 32
KV_HEADS = 8
HD = 128
BLOCK = 512
KMAX = 256
GROUP = HEADS // KV_HEADS
N_Z = 8
N_Y = 8
N_X = 4
STRIP = D // (N_Z * N_Y)
HALF = N_Y // 2 * STRIP
QW = GROUP * HD
KVW = 2 * HD
LOG2E = 1.4426950408889634
SCALE = HD**-0.5 * LOG2E
NEG = -1e30
VMEM_LIMIT = 48 * 1024 * 1024

Z_GROUPS = [[z * N_Y + y for z in range(N_Z)] for y in range(N_Y)]
X_GROUPS = [[2 * x + c for x in range(N_X)] for c in range(2)]
CORE_SWAP = [(i, i ^ 1) for i in range(2 * N_X)]
SIBLING_SWAP = [(i, i ^ 1) for i in range(N_Z * N_Y)]
PARITY_GROUPS = [[z * N_Y + 2 * p + q for p in range(N_Y // 2)] for z in range(N_Z) for q in range(2)]


def params():
    return pltpu.CompilerParams(vmem_limit_bytes=VMEM_LIMIT)


def dot(a, b):
    return jnp.dot(a, b, preferred_element_type=jnp.float32)


def dot_t(a, b):
    return lax.dot_general(a, b, (((1,), (1,)), ((), ())), preferred_element_type=jnp.float32)


def attend(scores, values):
    top = jnp.max(scores, axis=1, keepdims=True)
    unnormed = jnp.exp2(scores - top)
    total = jnp.sum(unnormed, axis=1, keepdims=True)
    return dot(unnormed.astype(jnp.bfloat16), values) / total


def lower_kernel(index_ref, q_ref, k_ref, v_ref, hidden_ref, gain_ref, inverse_ref, out_ref):
    index = index_ref[...]
    column = lax.broadcasted_iota(jnp.int32, (KMAX, BLOCK), 1)
    pick = (column == index).astype(jnp.bfloat16)
    causal = column <= index
    queries = dot(pick, q_ref[...]).astype(jnp.bfloat16)
    keys = k_ref[...]
    values = v_ref[...]
    for g in range(GROUP):
        cols = slice(g * HD, (g + 1) * HD)
        scores = jnp.where(causal, dot_t(queries[:, cols], keys) * SCALE, NEG)
        out_ref[:, cols] = attend(scores, values).astype(jnp.bfloat16)
    out_ref[:, QW:] = dot(pick, hidden_ref[...]).astype(jnp.bfloat16)


def lower(index, queries, keys, values, hidden, gain, inverse):
    return pl.pallas_call(
        lower_kernel,
        in_specs=[pl.BlockSpec(memory_space=pltpu.VMEM)] * 5 + [pl.BlockSpec(memory_space=pl.ANY)] * 2,
        out_shape=jax.ShapeDtypeStruct((KMAX, 2 * QW), jnp.bfloat16),
        compiler_params=params(),
        name="lower",
    )(index, queries, keys, values, hidden, gain, inverse)


def project_kernel(other, place_ref, own_ref, pair_ref, weight_ref, out_ref):
    core = 1 - place_ref[0] if other else place_ref[0]
    own = own_ref[:, :QW]
    pair = pair_ref[:, :QW]
    for x in range(N_X):
        weights = weight_ref[2 * x + core]
        out_ref[x, :KMAX] = dot_t(own, weights).astype(out_ref.dtype)
        out_ref[x, KMAX:] = dot_t(pair, weights).astype(out_ref.dtype)


def project(place, kept, kept_pair, weights, other):
    return pl.pallas_call(
        functools.partial(project_kernel, other),
        in_specs=[pl.BlockSpec(memory_space=pltpu.SMEM)] + [pl.BlockSpec(memory_space=pltpu.VMEM)] * 3,
        out_specs=pl.BlockSpec(memory_space=pltpu.VMEM),
        out_shape=jax.ShapeDtypeStruct(
            (N_X, 2 * KMAX, HALF), jnp.bfloat16 if other else jnp.float32
        ),
        compiler_params=params(),
        cost_estimate=pl.CostEstimate(flops=2**30 // 2, bytes_accessed=2**20, transcendentals=0),
        name="project_other" if other else "project_mine",
    )(place, kept, kept_pair, weights)


def state_kernel(place_ref, parts_ref, hid_ref, hid_pair_ref, gain_ref, out_ref):
    gain = gain_ref[place_ref[4]]
    parity = place_ref[1]
    row = lax.broadcasted_iota(jnp.int32, (QW, HALF), 0)
    col = lax.broadcasted_iota(jnp.int32, (QW, HALF), 1)
    source = (col // STRIP) * (2 * STRIP) + parity * STRIP + col % STRIP
    pick = (row == source).astype(jnp.bfloat16)
    for half, hid in enumerate((hid_ref, hid_pair_ref)):
        rows = slice(half * KMAX, (half + 1) * KMAX)
        total = dot(hid[...], pick)
        for x in range(N_X):
            total += parts_ref[x, rows].astype(jnp.float32)
        state = total.astype(jnp.bfloat16).astype(jnp.float32)
        scaled = (state * gain).astype(jnp.bfloat16)
        for x in range(N_X):
            out_ref[x, rows] = scaled


def add_up(place, parts, kept, kept_pair, gain):
    shape = (N_X, 2 * KMAX, HALF)
    hidden = pl.BlockSpec((KMAX, QW), lambda i: (0, 1))
    return pl.pallas_call(
        state_kernel,
        grid=(1,),
        in_specs=[
            pl.BlockSpec(memory_space=pltpu.SMEM),
            pl.BlockSpec(shape, lambda i: (0, 0, 0)),
            hidden,
            hidden,
            pl.BlockSpec((2 * N_X, 1, HALF), lambda i: (0, 0, 0)),
        ],
        out_specs=pl.BlockSpec(shape, lambda i: (0, 0, 0)),
        out_shape=jax.ShapeDtypeStruct(shape, jnp.bfloat16),
        compiler_params=params(),
        name="state",
    )(place, parts, kept, kept_pair, gain)


def by_core(core):
    return [2 * x + core for x in range(N_X)] + [2 * x + 1 - core for x in range(N_X)]


OWN = slice(0, KMAX)
PAIR = slice(KMAX, 2 * KMAX)


def contract(rows, mine_ref, other_ref, weights):
    state = [ref[x, rows] for ref in (mine_ref, other_ref) for x in range(N_X)]
    return dot(jnp.concatenate(state, axis=1), weights)


def kv_kernel(place_ref, mine_ref, other_ref, weight_ref, keep_ref, send_ref):
    heads = by_core(place_ref[0])
    weights = jnp.concatenate([weight_ref[head, :, QW:] for head in heads], axis=0)
    for half, rows in enumerate((OWN, PAIR)):
        sums = contract(rows, mine_ref, other_ref, weights)
        keep_ref[rows] = sums
        send_ref[:, (1 - half) * KVW : (2 - half) * KVW] = sums.astype(jnp.bfloat16)
    weights = jnp.concatenate([weight_ref[head, :, :HD] for head in heads], axis=0)
    sums = contract(PAIR, mine_ref, other_ref, weights)
    send_ref[:, 2 * KVW :] = sums.astype(jnp.bfloat16)


def project_kv(place, mine, other, weights):
    return pl.pallas_call(
        kv_kernel,
        in_specs=[pl.BlockSpec(memory_space=pltpu.SMEM)] + [pl.BlockSpec(memory_space=pltpu.VMEM)] * 3,
        out_specs=[pl.BlockSpec(memory_space=pltpu.VMEM)] * 2,
        out_shape=[
            jax.ShapeDtypeStruct((2 * KMAX, KVW), jnp.float32),
            jax.ShapeDtypeStruct((KMAX, 2 * KVW + HD), jnp.bfloat16),
        ],
        compiler_params=params(),
        name="project_kv",
    )(place, mine, other, weights)


def q_kernel(
    place_ref, mine_ref, other_ref, weight_ref, inverse_ref, first_ref, keep_ref, square_ref, send_ref
):
    heads = by_core(place_ref[0])
    weights = jnp.concatenate([weight_ref[head, :, HD:QW] for head in heads], axis=0)
    sums = contract(PAIR, mine_ref, other_ref, weights)
    send_ref[:, : QW - HD] = sums.astype(jnp.bfloat16)
    squares = jnp.zeros((2 * KMAX, HD), jnp.float32)
    for i, head in enumerate(heads):
        scaled = (mine_ref if i < N_X else other_ref)[i % N_X].astype(jnp.float32)
        square = scaled * scaled * inverse_ref[head]
        squares += square[:, :HD] + square[:, HD:]
    total = jnp.sum(squares, axis=1, keepdims=True)
    square_ref[...] = jnp.broadcast_to(total, square_ref.shape)
    high = total.astype(jnp.bfloat16).astype(jnp.float32)
    low = total - high
    lane = lax.broadcasted_iota(jnp.int32, (KMAX, HD), 1)
    tail = jnp.where(
        lane == 0,
        high[PAIR],
        jnp.where(lane == 1, low[PAIR], jnp.where(lane == 2, high[OWN], low[OWN])),
    )
    send_ref[:, QW - HD :] = tail.astype(jnp.bfloat16)
    weights = jnp.concatenate([weight_ref[head, :, :QW] for head in heads], axis=0)
    keep_ref[...] = contract(OWN, mine_ref, other_ref, weights)


def project_q(place, mine, other, weights, inverse, first):
    return pl.pallas_call(
        q_kernel,
        in_specs=[pl.BlockSpec(memory_space=pltpu.SMEM)]
        + [pl.BlockSpec(memory_space=pltpu.VMEM)] * 4
        + [pl.BlockSpec(memory_space=pl.ANY)],
        out_specs=[pl.BlockSpec(memory_space=pltpu.VMEM)] * 3,
        out_shape=[
            jax.ShapeDtypeStruct((KMAX, QW), jnp.float32),
            jax.ShapeDtypeStruct((2 * KMAX, HD), jnp.float32),
            jax.ShapeDtypeStruct((KMAX, QW), jnp.bfloat16),
        ],
        compiler_params=params(),
        cost_estimate=pl.CostEstimate(flops=2**30, bytes_accessed=2**22, transcendentals=0),
        name="project_q",
    )(place, mine, other, weights, inverse, first)


def upper_kernel(place_ref, q_ref, kv_ref, square_ref, got_q_ref, got_kv_ref, out_ref):
    parity = place_ref[1]
    own_count = place_ref[2]
    left_count = place_ref[3]
    tail = got_q_ref[:, QW - HD :].astype(jnp.float32)
    own_sum = square_ref[:KMAX, :1] + (tail[:, 0:1] + tail[:, 1:2])
    pair_sum = square_ref[KMAX:, :1] + (tail[:, 2:3] + tail[:, 3:4])
    own_inv = lax.rsqrt(own_sum / D + 1e-05)
    pair_inv = lax.rsqrt(pair_sum / D + 1e-05)
    got = jnp.concatenate([got_kv_ref[:, 2 * KVW :], got_q_ref[:, : QW - HD]], axis=1)
    queries = ((q_ref[...] + got.astype(jnp.float32)) * own_inv).astype(jnp.bfloat16)
    own = (kv_ref[:KMAX] + got_kv_ref[:, :KVW].astype(jnp.float32)) * own_inv
    own = own.astype(jnp.bfloat16)
    pair = (kv_ref[KMAX:] + got_kv_ref[:, KVW : 2 * KVW].astype(jnp.float32)) * pair_inv
    pair = pair.astype(jnp.bfloat16)
    keys = jnp.concatenate([pair[:, :HD], own[:, :HD]], axis=0)
    values = jnp.concatenate([pair[:, HD:], own[:, HD:]], axis=0)
    row = lax.broadcasted_iota(jnp.int32, (KMAX, 2 * KMAX), 0)
    col = lax.broadcasted_iota(jnp.int32, (KMAX, 2 * KMAX), 1)
    from_left = col < left_count * parity
    from_own = (col >= KMAX) & (col - KMAX <= row) & (col - KMAX < own_count)
    allowed = from_left | from_own
    valid = lax.broadcasted_iota(jnp.int32, (KMAX, HD), 0) < own_count
    for g in range(GROUP):
        cols = slice(g * HD, (g + 1) * HD)
        scores = jnp.where(allowed, dot_t(queries[:, cols], keys) * SCALE, NEG)
        out_ref[:, cols] = jnp.where(valid, attend(scores, values), 0.0).astype(jnp.bfloat16)


def upper(place, q, kv, squares, got_q, got_kv):
    return pl.pallas_call(
        upper_kernel,
        in_specs=[pl.BlockSpec(memory_space=pltpu.SMEM)] + [pl.BlockSpec(memory_space=pltpu.VMEM)] * 5,
        out_shape=jax.ShapeDtypeStruct((KMAX, QW), jnp.bfloat16),
        compiler_params=params(),
        name="upper",
    )(place, q, kv, squares, got_q, got_kv)


def gather_head(x):
    mine = lax.all_to_all(x, "head", 0, 0, axis_index_groups=X_GROUPS, tiled=True)
    return mine, lax.ppermute(mine, "head", CORE_SWAP)


def per_device(
    hidden,
    queries,
    keys_low,
    values_low,
    out_weight,
    norm_gain,
    query_weight,
    key_weight,
    value_weight,
    keep_index,
    keep_count,
):
    seq = lax.axis_index("seq")
    parity = seq % 2
    head = lax.axis_index("head")
    core = head % 2
    own_count = lax.dynamic_index_in_dim(keep_count, seq, keepdims=False)
    left_count = lax.dynamic_index_in_dim(keep_count, jnp.maximum(seq - 1, 0), keepdims=False)
    place = jnp.stack([core, parity, own_count, left_count, head]).astype(jnp.int32)

    shard = out_weight.T
    shards = lax.all_to_all(
        jnp.broadcast_to(shard, (N_Y // 2,) + shard.shape),
        "seq",
        0,
        0,
        axis_index_groups=PARITY_GROUPS,
        tiled=True,
    )
    out_weights = lax.all_gather(
        shards.reshape(HALF, QW), "seq", axis=0, axis_index_groups=Z_GROUPS
    )

    gain = lax.dynamic_index_in_dim(
        norm_gain.reshape(8, N_Y // 2, 2, STRIP), parity, axis=2, keepdims=False
    ).reshape(8, 1, HALF)
    inverse = 1.0 / (gain * gain)
    index = keep_index.reshape(KMAX, 1)
    kept = lower(index, queries, keys_low, values_low, hidden, gain, inverse)
    kept_pair = lax.ppermute(kept, "seq", SIBLING_SWAP)

    shard = jnp.concatenate([query_weight, key_weight, value_weight], axis=1)
    shards = lax.all_gather(shard, "seq", axis=0, axis_index_groups=PARITY_GROUPS, tiled=True)
    qkv_weights = lax.all_gather(shards, "seq", axis=0, axis_index_groups=Z_GROUPS)

    send = project(place, kept, kept_pair, out_weights, True)
    got = lax.ppermute(send, "head", CORE_SWAP)
    keep = project(place, kept, kept_pair, out_weights, False)
    parts = (keep + got.astype(jnp.float32)).astype(jnp.bfloat16)
    parts = lax.all_to_all(parts, "head", 0, 0, axis_index_groups=X_GROUPS, tiled=True)
    mine, other = gather_head(add_up(place, parts, kept, kept_pair, gain))

    kv, send = project_kv(place, mine, other, qkv_weights)
    got_kv = lax.ppermute(send, "seq", SIBLING_SWAP)
    q, squares, send = project_q(place, mine, other, qkv_weights, inverse, kv)
    got_q = lax.ppermute(send, "seq", SIBLING_SWAP)
    return upper(place, q, kv, squares, got_q, got_kv)


def solution(mesh):
    in_specs = (
        P("seq", "head"),
        P("seq", "head"),
        P("seq", "head"),
        P("seq", "head"),
        P("head", "seq"),
        P(),
        P("seq", "head"),
        P("seq", "head"),
        P("seq", "head"),
        P("seq", None),
        P(),
    )
    out_specs = P("seq", "head")
    return jax.shard_map(
        per_device, mesh=mesh, in_specs=in_specs, out_specs=out_specs, check_vma=False
    )
```

```python
import functools

import jax
import jax.numpy as jnp
from jax import lax
from jax.experimental import pallas as pl
from jax.experimental.pallas import tpu as pltpu
from jax.sharding import PartitionSpec as P

D = 4096
HEADS = 32
KV_HEADS = 8
HD = 128
BLOCK = 512
KMAX = 256
GROUP = HEADS // KV_HEADS
N_Z = 8
N_Y = 8
N_X = 4
TAIL = 16
STRIP = D // (N_Z * N_Y)
HALF = N_Y // 2 * STRIP
QW = GROUP * HD
KVW = 2 * HD
LOG2E = 1.4426950408889634
SCALE = HD**-0.5 * LOG2E
NEG = -1e30
VMEM_LIMIT = 48 * 1024 * 1024

Z_GROUPS = [[z * N_Y + y for z in range(N_Z)] for y in range(N_Y)]
X_GROUPS = [[2 * x + c for x in range(N_X)] for c in range(2)]
CORE_SWAP = [(i, i ^ 1) for i in range(2 * N_X)]
SIBLING_SWAP = [(i, i ^ 1) for i in range(N_Z * N_Y)]
PARITY_GROUPS = [[z * N_Y + 2 * p + q for p in range(N_Y // 2)] for z in range(N_Z) for q in range(2)]


def params():
    return pltpu.CompilerParams(vmem_limit_bytes=VMEM_LIMIT)


def dot(a, b):
    return jnp.dot(a, b, preferred_element_type=jnp.float32)


def dot_t(a, b):
    return lax.dot_general(a, b, (((1,), (1,)), ((), ())), preferred_element_type=jnp.float32)


def attend(scores, values):
    top = jnp.max(scores, axis=1, keepdims=True)
    unnormed = jnp.exp2(scores - top)
    total = jnp.sum(unnormed, axis=1, keepdims=True)
    return dot(unnormed.astype(jnp.bfloat16), values) / total


def lower_kernel(index_ref, q_ref, k_ref, v_ref, hidden_ref, gain_ref, inverse_ref, out_ref):
    index = index_ref[...]
    column = lax.broadcasted_iota(jnp.int32, (KMAX, BLOCK), 1)
    pick = (column == index).astype(jnp.bfloat16)
    causal = column <= index
    queries = dot(pick, q_ref[...]).astype(jnp.bfloat16)
    keys = k_ref[...]
    values = v_ref[...]
    for g in range(GROUP):
        cols = slice(g * HD, (g + 1) * HD)
        scores = jnp.where(causal, dot_t(queries[:, cols], keys) * SCALE, NEG)
        out_ref[:, cols] = attend(scores, values).astype(jnp.bfloat16)
    out_ref[:, QW:] = dot(pick, hidden_ref[...]).astype(jnp.bfloat16)


def lower(index, queries, keys, values, hidden, gain, inverse):
    return pl.pallas_call(
        lower_kernel,
        in_specs=[pl.BlockSpec(memory_space=pltpu.VMEM)] * 5 + [pl.BlockSpec(memory_space=pl.ANY)] * 2,
        out_shape=jax.ShapeDtypeStruct((KMAX, 2 * QW), jnp.bfloat16),
        compiler_params=params(),
        name="lower",
    )(index, queries, keys, values, hidden, gain, inverse)


def project_kernel(other, place_ref, own_ref, pair_ref, weight_ref, out_ref):
    core = 1 - place_ref[0] if other else place_ref[0]
    own = own_ref[:, :QW]
    pair = pair_ref[:, :QW]
    for x in range(N_X):
        weights = weight_ref[2 * x + core]
        out_ref[x, :KMAX] = dot_t(own, weights).astype(out_ref.dtype)
        out_ref[x, KMAX:] = dot_t(pair, weights).astype(out_ref.dtype)


def project(place, kept, kept_pair, weights, other):
    return pl.pallas_call(
        functools.partial(project_kernel, other),
        in_specs=[pl.BlockSpec(memory_space=pltpu.SMEM)] + [pl.BlockSpec(memory_space=pltpu.VMEM)] * 3,
        out_specs=pl.BlockSpec(memory_space=pltpu.VMEM),
        out_shape=jax.ShapeDtypeStruct(
            (N_X, 2 * KMAX, HALF), jnp.bfloat16 if other else jnp.float32
        ),
        compiler_params=params(),
        cost_estimate=pl.CostEstimate(flops=2**30 // 2, bytes_accessed=2**20, transcendentals=0),
        name="project_other" if other else "project_mine",
    )(place, kept, kept_pair, weights)


def state_kernel(place_ref, parts_ref, hid_ref, hid_pair_ref, gain_ref, out_ref):
    gain = gain_ref[place_ref[4]]
    parity = place_ref[1]
    row = lax.broadcasted_iota(jnp.int32, (QW, HALF), 0)
    col = lax.broadcasted_iota(jnp.int32, (QW, HALF), 1)
    source = (col // STRIP) * (2 * STRIP) + parity * STRIP + col % STRIP
    pick = (row == source).astype(jnp.bfloat16)
    for half, hid in enumerate((hid_ref, hid_pair_ref)):
        rows = slice(half * KMAX, (half + 1) * KMAX)
        total = dot(hid[...], pick)
        for x in range(N_X):
            total += parts_ref[x, rows].astype(jnp.float32)
        state = total.astype(jnp.bfloat16).astype(jnp.float32)
        scaled = (state * gain).astype(jnp.bfloat16)
        for x in range(N_X):
            out_ref[x, rows] = scaled


def add_up(place, parts, kept, kept_pair, gain):
    shape = (N_X, 2 * KMAX, HALF)
    hidden = pl.BlockSpec((KMAX, QW), lambda i: (0, 1))
    return pl.pallas_call(
        state_kernel,
        grid=(1,),
        in_specs=[
            pl.BlockSpec(memory_space=pltpu.SMEM),
            pl.BlockSpec(shape, lambda i: (0, 0, 0)),
            hidden,
            hidden,
            pl.BlockSpec((2 * N_X, 1, HALF), lambda i: (0, 0, 0)),
        ],
        out_specs=pl.BlockSpec(shape, lambda i: (0, 0, 0)),
        out_shape=jax.ShapeDtypeStruct(shape, jnp.bfloat16),
        compiler_params=params(),
        name="state",
    )(place, parts, kept, kept_pair, gain)


def by_core(core):
    return [2 * x + core for x in range(N_X)] + [2 * x + 1 - core for x in range(N_X)]


OWN = slice(0, KMAX)
PAIR = slice(KMAX, 2 * KMAX)


def contract(rows, mine_ref, other_ref, weights):
    state = [ref[x, rows] for ref in (mine_ref, other_ref) for x in range(N_X)]
    return dot(jnp.concatenate(state, axis=1), weights)


def kv_kernel(place_ref, mine_ref, other_ref, weight_ref, keep_ref, send_ref):
    heads = by_core(place_ref[0])
    weights = jnp.concatenate([weight_ref[head, :, QW:] for head in heads], axis=0)
    for half, rows in enumerate((OWN, PAIR)):
        sums = contract(rows, mine_ref, other_ref, weights)
        keep_ref[rows] = sums
        send_ref[:, (1 - half) * KVW : (2 - half) * KVW] = sums.astype(jnp.bfloat16)
    weights = jnp.concatenate([weight_ref[head, :, :HD] for head in heads], axis=0)
    sums = contract(PAIR, mine_ref, other_ref, weights)
    send_ref[:, 2 * KVW :] = sums.astype(jnp.bfloat16)


def project_kv(place, mine, other, weights):
    return pl.pallas_call(
        kv_kernel,
        in_specs=[pl.BlockSpec(memory_space=pltpu.SMEM)] + [pl.BlockSpec(memory_space=pltpu.VMEM)] * 3,
        out_specs=[pl.BlockSpec(memory_space=pltpu.VMEM)] * 2,
        out_shape=[
            jax.ShapeDtypeStruct((2 * KMAX, KVW), jnp.float32),
            jax.ShapeDtypeStruct((KMAX, 2 * KVW + HD), jnp.bfloat16),
        ],
        compiler_params=params(),
        name="project_kv",
    )(place, mine, other, weights)


def sibling_kernel(
    place_ref, mine_ref, other_ref, weight_ref, inverse_ref, first_ref, square_ref, send_ref
):
    heads = by_core(place_ref[0])
    weights = jnp.concatenate([weight_ref[head, :, HD:QW] for head in heads], axis=0)
    sums = contract(PAIR, mine_ref, other_ref, weights)
    send_ref[:KMAX] = sums.astype(jnp.bfloat16)
    squares = jnp.zeros((2 * KMAX, HD), jnp.float32)
    for i, head in enumerate(heads):
        scaled = (mine_ref if i < N_X else other_ref)[i % N_X].astype(jnp.float32)
        square = scaled * scaled * inverse_ref[head]
        squares += square[:, :HD] + square[:, HD:]
    total = jnp.sum(squares, axis=1, keepdims=True)
    square_ref[...] = jnp.broadcast_to(total, square_ref.shape)
    across = lax.dot_general(
        jnp.ones((TAIL, HD), jnp.float32),
        squares,
        (((1,), (1,)), ((), ())),
        precision=lax.Precision.HIGHEST,
        preferred_element_type=jnp.float32,
    )
    high = across.astype(jnp.bfloat16).astype(jnp.float32)
    low = across - high
    row = lax.broadcasted_iota(jnp.int32, (TAIL, KMAX), 0)
    tail = jnp.where(
        row == 0,
        high[:, PAIR],
        jnp.where(row == 1, low[:, PAIR], jnp.where(row == 2, high[:, OWN], low[:, OWN])),
    )
    send_ref[KMAX:] = jnp.concatenate([tail, tail[:, :HD]], axis=1).astype(jnp.bfloat16)


def project_sibling(place, mine, other, weights, inverse, first):
    return pl.pallas_call(
        sibling_kernel,
        in_specs=[pl.BlockSpec(memory_space=pltpu.SMEM)]
        + [pl.BlockSpec(memory_space=pltpu.VMEM)] * 4
        + [pl.BlockSpec(memory_space=pl.ANY)],
        out_specs=[pl.BlockSpec(memory_space=pltpu.VMEM)] * 2,
        out_shape=[
            jax.ShapeDtypeStruct((2 * KMAX, HD), jnp.float32),
            jax.ShapeDtypeStruct((KMAX + TAIL, QW - HD), jnp.bfloat16),
        ],
        compiler_params=params(),
        cost_estimate=pl.CostEstimate(flops=2**29, bytes_accessed=2**22, transcendentals=0),
        name="project_sibling",
    )(place, mine, other, weights, inverse, first)


def q_kernel(place_ref, mine_ref, other_ref, weight_ref, first_ref, out_ref):
    heads = by_core(place_ref[0])
    weights = jnp.concatenate([weight_ref[head, :, :QW] for head in heads], axis=0)
    out_ref[...] = contract(OWN, mine_ref, other_ref, weights)


def project_q(place, mine, other, weights, first):
    return pl.pallas_call(
        q_kernel,
        in_specs=[pl.BlockSpec(memory_space=pltpu.SMEM)]
        + [pl.BlockSpec(memory_space=pltpu.VMEM)] * 3
        + [pl.BlockSpec(memory_space=pl.ANY)],
        out_specs=pl.BlockSpec(memory_space=pltpu.VMEM),
        out_shape=jax.ShapeDtypeStruct((KMAX, QW), jnp.float32),
        compiler_params=params(),
        cost_estimate=pl.CostEstimate(flops=2**29, bytes_accessed=2**22, transcendentals=0),
        name="project_q",
    )(place, mine, other, weights, first)


def upper_kernel(place_ref, q_ref, kv_ref, square_ref, got_q_ref, got_kv_ref, out_ref):
    parity = place_ref[1]
    own_count = place_ref[2]
    left_count = place_ref[3]
    tail = got_q_ref[KMAX:, :KMAX].astype(jnp.float32)
    same = lax.broadcasted_iota(jnp.int32, (KMAX, KMAX), 0) == lax.broadcasted_iota(
        jnp.int32, (KMAX, KMAX), 1
    )

    def down(across):
        return jnp.sum(jnp.where(same, across, 0.0), axis=1, keepdims=True)

    own_sum = square_ref[:KMAX, :1] + down(tail[0:1] + tail[1:2])
    pair_sum = square_ref[KMAX:, :1] + down(tail[2:3] + tail[3:4])
    own_inv = lax.rsqrt(own_sum / D + 1e-05)
    pair_inv = lax.rsqrt(pair_sum / D + 1e-05)
    got = jnp.concatenate([got_kv_ref[:, 2 * KVW :], got_q_ref[:KMAX]], axis=1)
    queries = ((q_ref[...] + got.astype(jnp.float32)) * own_inv).astype(jnp.bfloat16)
    own = (kv_ref[:KMAX] + got_kv_ref[:, :KVW].astype(jnp.float32)) * own_inv
    own = own.astype(jnp.bfloat16)
    pair = (kv_ref[KMAX:] + got_kv_ref[:, KVW : 2 * KVW].astype(jnp.float32)) * pair_inv
    pair = pair.astype(jnp.bfloat16)
    keys = jnp.concatenate([pair[:, :HD], own[:, :HD]], axis=0)
    values = jnp.concatenate([pair[:, HD:], own[:, HD:]], axis=0)
    row = lax.broadcasted_iota(jnp.int32, (KMAX, 2 * KMAX), 0)
    col = lax.broadcasted_iota(jnp.int32, (KMAX, 2 * KMAX), 1)
    from_left = col < left_count * parity
    from_own = (col >= KMAX) & (col - KMAX <= row) & (col - KMAX < own_count)
    allowed = from_left | from_own
    valid = lax.broadcasted_iota(jnp.int32, (KMAX, HD), 0) < own_count
    for g in range(GROUP):
        cols = slice(g * HD, (g + 1) * HD)
        scores = jnp.where(allowed, dot_t(queries[:, cols], keys) * SCALE, NEG)
        out_ref[:, cols] = jnp.where(valid, attend(scores, values), 0.0).astype(jnp.bfloat16)


def upper(place, q, kv, squares, got_q, got_kv):
    return pl.pallas_call(
        upper_kernel,
        in_specs=[pl.BlockSpec(memory_space=pltpu.SMEM)] + [pl.BlockSpec(memory_space=pltpu.VMEM)] * 5,
        out_shape=jax.ShapeDtypeStruct((KMAX, QW), jnp.bfloat16),
        compiler_params=params(),
        name="upper",
    )(place, q, kv, squares, got_q, got_kv)


def gather_head(x):
    mine = lax.all_to_all(x, "head", 0, 0, axis_index_groups=X_GROUPS, tiled=True)
    return mine, lax.ppermute(mine, "head", CORE_SWAP)


def per_device(
    hidden,
    queries,
    keys_low,
    values_low,
    out_weight,
    norm_gain,
    query_weight,
    key_weight,
    value_weight,
    keep_index,
    keep_count,
):
    seq = lax.axis_index("seq")
    parity = seq % 2
    head = lax.axis_index("head")
    core = head % 2
    own_count = lax.dynamic_index_in_dim(keep_count, seq, keepdims=False)
    left_count = lax.dynamic_index_in_dim(keep_count, jnp.maximum(seq - 1, 0), keepdims=False)
    place = jnp.stack([core, parity, own_count, left_count, head]).astype(jnp.int32)

    shard = out_weight.T
    shards = lax.all_to_all(
        jnp.broadcast_to(shard, (N_Y // 2,) + shard.shape),
        "seq",
        0,
        0,
        axis_index_groups=PARITY_GROUPS,
        tiled=True,
    )
    out_weights = lax.all_gather(
        shards.reshape(HALF, QW), "seq", axis=0, axis_index_groups=Z_GROUPS
    )

    gain = lax.dynamic_index_in_dim(
        norm_gain.reshape(8, N_Y // 2, 2, STRIP), parity, axis=2, keepdims=False
    ).reshape(8, 1, HALF)
    inverse = 1.0 / (gain * gain)
    index = keep_index.reshape(KMAX, 1)
    kept = lower(index, queries, keys_low, values_low, hidden, gain, inverse)
    kept_pair = lax.ppermute(kept, "seq", SIBLING_SWAP)

    shard = jnp.concatenate([query_weight, key_weight, value_weight], axis=1)
    shards = lax.all_gather(shard, "seq", axis=0, axis_index_groups=PARITY_GROUPS, tiled=True)
    qkv_weights = lax.all_gather(shards, "seq", axis=0, axis_index_groups=Z_GROUPS)

    send = project(place, kept, kept_pair, out_weights, True)
    got = lax.ppermute(send, "head", CORE_SWAP)
    keep = project(place, kept, kept_pair, out_weights, False)
    parts = (keep + got.astype(jnp.float32)).astype(jnp.bfloat16)
    parts = lax.all_to_all(parts, "head", 0, 0, axis_index_groups=X_GROUPS, tiled=True)
    mine, other = gather_head(add_up(place, parts, kept, kept_pair, gain))

    kv, send = project_kv(place, mine, other, qkv_weights)
    got_kv = lax.ppermute(send, "seq", SIBLING_SWAP)
    squares, send = project_sibling(place, mine, other, qkv_weights, inverse, kv)
    got_q = lax.ppermute(send, "seq", SIBLING_SWAP)
    q = project_q(place, mine, other, qkv_weights, send)
    return upper(place, q, kv, squares, got_q, got_kv)


def solution(mesh):
    in_specs = (
        P("seq", "head"),
        P("seq", "head"),
        P("seq", "head"),
        P("seq", "head"),
        P("head", "seq"),
        P(),
        P("seq", "head"),
        P("seq", "head"),
        P("seq", "head"),
        P("seq", None),
        P(),
    )
    out_specs = P("seq", "head")
    return jax.shard_map(
        per_device, mesh=mesh, in_specs=in_specs, out_specs=out_specs, check_vma=False
    )
```

```python
import functools

import jax
import jax.numpy as jnp
from jax import lax
from jax.experimental import pallas as pl
from jax.experimental.pallas import tpu as pltpu
from jax.sharding import PartitionSpec as P

D = 4096
HEADS = 32
KV_HEADS = 8
HD = 128
BLOCK = 512
KMAX = 256
GROUP = HEADS // KV_HEADS
N_Z = 8
N_Y = 8
N_X = 4
TAIL = 16
STRIP = D // (N_Z * N_Y)
HALF = N_Y // 2 * STRIP
QW = GROUP * HD
KVW = 2 * HD
LOG2E = 1.4426950408889634
SCALE = HD**-0.5 * LOG2E
NEG = -1e30
VMEM_LIMIT = 48 * 1024 * 1024

Z_GROUPS = [[z * N_Y + y for z in range(N_Z)] for y in range(N_Y)]
X_GROUPS = [[2 * x + c for x in range(N_X)] for c in range(2)]
CORE_SWAP = [(i, i ^ 1) for i in range(2 * N_X)]
SIBLING_SWAP = [(i, i ^ 1) for i in range(N_Z * N_Y)]
PARITY_GROUPS = [[z * N_Y + 2 * p + q for p in range(N_Y // 2)] for z in range(N_Z) for q in range(2)]


def params():
    return pltpu.CompilerParams(vmem_limit_bytes=VMEM_LIMIT)


def dot(a, b):
    return jnp.dot(a, b, preferred_element_type=jnp.float32)


def dot_t(a, b):
    return lax.dot_general(a, b, (((1,), (1,)), ((), ())), preferred_element_type=jnp.float32)


def with_ones(values):
    return jnp.concatenate([values, jnp.ones_like(values)], axis=1)


def attend(scores, values):
    top = jnp.max(scores, axis=1, keepdims=True)
    unnormed = jnp.exp2(scores - top).astype(jnp.bfloat16)
    sums = dot(unnormed, values)
    return sums[:, :HD] / sums[:, HD : HD + 1]


def lower_kernel(index_ref, q_ref, k_ref, v_ref, hidden_ref, gain_ref, inverse_ref, out_ref):
    index = index_ref[...]
    column = lax.broadcasted_iota(jnp.int32, (KMAX, BLOCK), 1)
    pick = (column == index).astype(jnp.bfloat16)
    causal = column <= index
    queries = dot(pick, q_ref[...]).astype(jnp.bfloat16)
    keys = k_ref[...]
    values = with_ones(v_ref[...])
    for g in range(GROUP):
        cols = slice(g * HD, (g + 1) * HD)
        scores = jnp.where(causal, dot_t(queries[:, cols], keys) * SCALE, NEG)
        out_ref[:, cols] = attend(scores, values).astype(jnp.bfloat16)
    out_ref[:, QW:] = dot(pick, hidden_ref[...]).astype(jnp.bfloat16)


def lower(index, queries, keys, values, hidden, gain, inverse):
    return pl.pallas_call(
        lower_kernel,
        in_specs=[pl.BlockSpec(memory_space=pltpu.VMEM)] * 5 + [pl.BlockSpec(memory_space=pl.ANY)] * 2,
        out_shape=jax.ShapeDtypeStruct((KMAX, 2 * QW), jnp.bfloat16),
        compiler_params=params(),
        name="lower",
    )(index, queries, keys, values, hidden, gain, inverse)


def project_kernel(other, place_ref, own_ref, pair_ref, weight_ref, out_ref):
    core = 1 - place_ref[0] if other else place_ref[0]
    own = own_ref[:, :QW]
    pair = pair_ref[:, :QW]
    for x in range(N_X):
        weights = weight_ref[2 * x + core]
        out_ref[x, :KMAX] = dot_t(own, weights).astype(out_ref.dtype)
        out_ref[x, KMAX:] = dot_t(pair, weights).astype(out_ref.dtype)


def project(place, kept, kept_pair, weights, other):
    return pl.pallas_call(
        functools.partial(project_kernel, other),
        in_specs=[pl.BlockSpec(memory_space=pltpu.SMEM)] + [pl.BlockSpec(memory_space=pltpu.VMEM)] * 3,
        out_specs=pl.BlockSpec(memory_space=pltpu.VMEM),
        out_shape=jax.ShapeDtypeStruct(
            (N_X, 2 * KMAX, HALF), jnp.bfloat16 if other else jnp.float32
        ),
        compiler_params=params(),
        cost_estimate=pl.CostEstimate(flops=2**30 // 2, bytes_accessed=2**20, transcendentals=0),
        name="project_other" if other else "project_mine",
    )(place, kept, kept_pair, weights)


def state_kernel(place_ref, parts_ref, hid_ref, hid_pair_ref, gain_ref, out_ref):
    gain = gain_ref[place_ref[4]]
    parity = place_ref[1]
    row = lax.broadcasted_iota(jnp.int32, (QW, HALF), 0)
    col = lax.broadcasted_iota(jnp.int32, (QW, HALF), 1)
    source = (col // STRIP) * (2 * STRIP) + parity * STRIP + col % STRIP
    pick = (row == source).astype(jnp.bfloat16)
    for half, hid in enumerate((hid_ref, hid_pair_ref)):
        rows = slice(half * KMAX, (half + 1) * KMAX)
        total = dot(hid[...], pick)
        for x in range(N_X):
            total += parts_ref[x, rows].astype(jnp.float32)
        state = total.astype(jnp.bfloat16).astype(jnp.float32)
        scaled = (state * gain).astype(jnp.bfloat16)
        for x in range(N_X):
            out_ref[x, rows] = scaled


def add_up(place, parts, kept, kept_pair, gain):
    shape = (N_X, 2 * KMAX, HALF)
    hidden = pl.BlockSpec((KMAX, QW), lambda i: (0, 1))
    return pl.pallas_call(
        state_kernel,
        grid=(1,),
        in_specs=[
            pl.BlockSpec(memory_space=pltpu.SMEM),
            pl.BlockSpec(shape, lambda i: (0, 0, 0)),
            hidden,
            hidden,
            pl.BlockSpec((2 * N_X, 1, HALF), lambda i: (0, 0, 0)),
        ],
        out_specs=pl.BlockSpec(shape, lambda i: (0, 0, 0)),
        out_shape=jax.ShapeDtypeStruct(shape, jnp.bfloat16),
        compiler_params=params(),
        name="state",
    )(place, parts, kept, kept_pair, gain)


def by_core(core):
    return [2 * x + core for x in range(N_X)] + [2 * x + 1 - core for x in range(N_X)]


OWN = slice(0, KMAX)
PAIR = slice(KMAX, 2 * KMAX)


def contract(rows, mine_ref, other_ref, weights):
    state = [ref[x, rows] for ref in (mine_ref, other_ref) for x in range(N_X)]
    return dot(jnp.concatenate(state, axis=1), weights)


def kv_kernel(place_ref, mine_ref, other_ref, weight_ref, keep_ref, send_ref, kv_ref, first_ref, sems):
    heads = by_core(place_ref[0])
    copies = []
    for cols, buffer in ((pl.ds(QW, KVW), kv_ref), (pl.ds(0, HD), first_ref)):
        for i, head in enumerate(heads):
            source = weight_ref.at[head, :, cols]
            copies.append(pltpu.make_async_copy(source, buffer.at[i], sems.at[len(copies)]))
            copies[-1].start()
    for copy in copies[: 2 * N_X]:
        copy.wait()
    weights = kv_ref[...].reshape(2 * N_X * HALF, KVW)
    for half, rows in enumerate((OWN, PAIR)):
        sums = contract(rows, mine_ref, other_ref, weights)
        keep_ref[rows] = sums
        send_ref[:, (1 - half) * KVW : (2 - half) * KVW] = sums.astype(jnp.bfloat16)
    for copy in copies[2 * N_X :]:
        copy.wait()
    sums = contract(PAIR, mine_ref, other_ref, first_ref[...].reshape(2 * N_X * HALF, HD))
    send_ref[:, 2 * KVW :] = sums.astype(jnp.bfloat16)


def project_kv(place, mine, other, weights):
    return pl.pallas_call(
        kv_kernel,
        in_specs=[
            pl.BlockSpec(memory_space=pltpu.SMEM),
            pl.BlockSpec(memory_space=pltpu.VMEM),
            pl.BlockSpec(memory_space=pltpu.VMEM),
            pl.BlockSpec(memory_space=pl.ANY),
        ],
        out_specs=[pl.BlockSpec(memory_space=pltpu.VMEM)] * 2,
        out_shape=[
            jax.ShapeDtypeStruct((2 * KMAX, KVW), jnp.float32),
            jax.ShapeDtypeStruct((KMAX, 2 * KVW + HD), jnp.bfloat16),
        ],
        scratch_shapes=[
            pltpu.VMEM((2 * N_X, HALF, KVW), jnp.bfloat16),
            pltpu.VMEM((2 * N_X, HALF, HD), jnp.bfloat16),
            pltpu.SemaphoreType.DMA((4 * N_X,)),
        ],
        compiler_params=pltpu.CompilerParams(vmem_limit_bytes=50 * 1024 * 1024),
        name="project_kv",
    )(place, mine, other, weights)


def sibling_kernel(
    place_ref, mine_ref, other_ref, weight_ref, inverse_ref, first_ref, square_ref, send_ref
):
    heads = by_core(place_ref[0])
    weights = jnp.concatenate([weight_ref[head, :, HD:QW] for head in heads], axis=0)
    sums = contract(PAIR, mine_ref, other_ref, weights)
    send_ref[:KMAX] = sums.astype(jnp.bfloat16)
    squares = jnp.zeros((2 * KMAX, HD), jnp.float32)
    for i, head in enumerate(heads):
        scaled = (mine_ref if i < N_X else other_ref)[i % N_X].astype(jnp.float32)
        square = scaled * scaled * inverse_ref[head]
        squares += square[:, :HD] + square[:, HD:]
    total = jnp.sum(squares, axis=1, keepdims=True)
    square_ref[...] = jnp.broadcast_to(total, square_ref.shape)
    across = lax.dot_general(
        jnp.ones((TAIL, HD), jnp.float32),
        squares,
        (((1,), (1,)), ((), ())),
        precision=lax.Precision.HIGHEST,
        preferred_element_type=jnp.float32,
    )
    high = across.astype(jnp.bfloat16).astype(jnp.float32)
    low = across - high
    row = lax.broadcasted_iota(jnp.int32, (TAIL, KMAX), 0)
    tail = jnp.where(
        row == 0,
        high[:, PAIR],
        jnp.where(row == 1, low[:, PAIR], jnp.where(row == 2, high[:, OWN], low[:, OWN])),
    )
    send_ref[KMAX:] = jnp.concatenate([tail, tail[:, :HD]], axis=1).astype(jnp.bfloat16)


def project_sibling(place, mine, other, weights, inverse, first):
    return pl.pallas_call(
        sibling_kernel,
        in_specs=[pl.BlockSpec(memory_space=pltpu.SMEM)]
        + [pl.BlockSpec(memory_space=pltpu.VMEM)] * 4
        + [pl.BlockSpec(memory_space=pl.ANY)],
        out_specs=[pl.BlockSpec(memory_space=pltpu.VMEM)] * 2,
        out_shape=[
            jax.ShapeDtypeStruct((2 * KMAX, HD), jnp.float32),
            jax.ShapeDtypeStruct((KMAX + TAIL, QW - HD), jnp.bfloat16),
        ],
        compiler_params=params(),
        cost_estimate=pl.CostEstimate(flops=2**29, bytes_accessed=2**22, transcendentals=0),
        name="project_sibling",
    )(place, mine, other, weights, inverse, first)


def q_kernel(place_ref, mine_ref, other_ref, weight_ref, first_ref, out_ref):
    heads = by_core(place_ref[0])
    weights = jnp.concatenate([weight_ref[head, :, :QW] for head in heads], axis=0)
    out_ref[...] = contract(OWN, mine_ref, other_ref, weights)


def project_q(place, mine, other, weights, first):
    return pl.pallas_call(
        q_kernel,
        in_specs=[pl.BlockSpec(memory_space=pltpu.SMEM)]
        + [pl.BlockSpec(memory_space=pltpu.VMEM)] * 3
        + [pl.BlockSpec(memory_space=pl.ANY)],
        out_specs=pl.BlockSpec(memory_space=pltpu.VMEM),
        out_shape=jax.ShapeDtypeStruct((KMAX, QW), jnp.float32),
        compiler_params=params(),
        cost_estimate=pl.CostEstimate(flops=2**29, bytes_accessed=2**22, transcendentals=0),
        name="project_q",
    )(place, mine, other, weights, first)


def upper_kernel(place_ref, q_ref, kv_ref, square_ref, got_q_ref, got_kv_ref, out_ref):
    parity = place_ref[1]
    own_count = place_ref[2]
    left_count = place_ref[3]
    tail = got_q_ref[KMAX:, :KMAX].astype(jnp.float32)
    same = lax.broadcasted_iota(jnp.int32, (KMAX, KMAX), 0) == lax.broadcasted_iota(
        jnp.int32, (KMAX, KMAX), 1
    )

    def down(across):
        return jnp.sum(jnp.where(same, across, 0.0), axis=1, keepdims=True)

    own_sum = square_ref[:KMAX, :1] + down(tail[0:1] + tail[1:2])
    pair_sum = square_ref[KMAX:, :1] + down(tail[2:3] + tail[3:4])
    own_inv = lax.rsqrt(own_sum / D + 1e-05)
    pair_inv = lax.rsqrt(pair_sum / D + 1e-05)
    got = jnp.concatenate([got_kv_ref[:, 2 * KVW :], got_q_ref[:KMAX]], axis=1)
    queries = ((q_ref[...] + got.astype(jnp.float32)) * own_inv).astype(jnp.bfloat16)
    own = (kv_ref[:KMAX] + got_kv_ref[:, :KVW].astype(jnp.float32)) * own_inv
    own = own.astype(jnp.bfloat16)
    pair = (kv_ref[KMAX:] + got_kv_ref[:, KVW : 2 * KVW].astype(jnp.float32)) * pair_inv
    pair = pair.astype(jnp.bfloat16)
    keys = jnp.concatenate([pair[:, :HD], own[:, :HD]], axis=0)
    values = with_ones(jnp.concatenate([pair[:, HD:], own[:, HD:]], axis=0))
    row = lax.broadcasted_iota(jnp.int32, (KMAX, 2 * KMAX), 0)
    col = lax.broadcasted_iota(jnp.int32, (KMAX, 2 * KMAX), 1)
    from_left = col < left_count * parity
    from_own = (col >= KMAX) & (col - KMAX <= row) & (col - KMAX < own_count)
    allowed = from_left | from_own
    valid = lax.broadcasted_iota(jnp.int32, (KMAX, HD), 0) < own_count
    for g in range(GROUP):
        cols = slice(g * HD, (g + 1) * HD)
        scores = jnp.where(allowed, dot_t(queries[:, cols], keys) * SCALE, NEG)
        out_ref[:, cols] = jnp.where(valid, attend(scores, values), 0.0).astype(jnp.bfloat16)


def upper(place, q, kv, squares, got_q, got_kv):
    return pl.pallas_call(
        upper_kernel,
        in_specs=[pl.BlockSpec(memory_space=pltpu.SMEM)] + [pl.BlockSpec(memory_space=pltpu.VMEM)] * 5,
        out_shape=jax.ShapeDtypeStruct((KMAX, QW), jnp.bfloat16),
        compiler_params=params(),
        name="upper",
    )(place, q, kv, squares, got_q, got_kv)


def gather_head(x):
    mine = lax.all_to_all(x, "head", 0, 0, axis_index_groups=X_GROUPS, tiled=True)
    return mine, lax.ppermute(mine, "head", CORE_SWAP)


def per_device(
    hidden,
    queries,
    keys_low,
    values_low,
    out_weight,
    norm_gain,
    query_weight,
    key_weight,
    value_weight,
    keep_index,
    keep_count,
):
    seq = lax.axis_index("seq")
    parity = seq % 2
    head = lax.axis_index("head")
    core = head % 2
    own_count = lax.dynamic_index_in_dim(keep_count, seq, keepdims=False)
    left_count = lax.dynamic_index_in_dim(keep_count, jnp.maximum(seq - 1, 0), keepdims=False)
    place = jnp.stack([core, parity, own_count, left_count, head]).astype(jnp.int32)

    shard = out_weight.T
    shards = lax.all_to_all(
        jnp.broadcast_to(shard, (N_Y // 2,) + shard.shape),
        "seq",
        0,
        0,
        axis_index_groups=PARITY_GROUPS,
        tiled=True,
    )
    out_weights = lax.all_gather(
        shards.reshape(HALF, QW), "seq", axis=0, axis_index_groups=Z_GROUPS
    )

    gain = lax.dynamic_index_in_dim(
        norm_gain.reshape(8, N_Y // 2, 2, STRIP), parity, axis=2, keepdims=False
    ).reshape(8, 1, HALF)
    inverse = 1.0 / (gain * gain)
    index = keep_index.reshape(KMAX, 1)
    kept = lower(index, queries, keys_low, values_low, hidden, gain, inverse)
    kept_pair = lax.ppermute(kept, "seq", SIBLING_SWAP)

    shard = jnp.concatenate([query_weight, key_weight, value_weight], axis=1)
    shards = lax.all_gather(shard, "seq", axis=0, axis_index_groups=PARITY_GROUPS, tiled=True)
    qkv_weights = lax.all_gather(shards, "seq", axis=0, axis_index_groups=Z_GROUPS)

    send = project(place, kept, kept_pair, out_weights, True)
    got = lax.ppermute(send, "head", CORE_SWAP)
    keep = project(place, kept, kept_pair, out_weights, False)
    parts = (keep + got.astype(jnp.float32)).astype(jnp.bfloat16)
    parts = lax.all_to_all(parts, "head", 0, 0, axis_index_groups=X_GROUPS, tiled=True)
    mine, other = gather_head(add_up(place, parts, kept, kept_pair, gain))

    kv, send = project_kv(place, mine, other, qkv_weights)
    got_kv = lax.ppermute(send, "seq", SIBLING_SWAP)
    squares, send = project_sibling(place, mine, other, qkv_weights, inverse, kv)
    got_q = lax.ppermute(send, "seq", SIBLING_SWAP)
    q = project_q(place, mine, other, qkv_weights, send)
    return upper(place, q, kv, squares, got_q, got_kv)


def solution(mesh):
    in_specs = (
        P("seq", "head"),
        P("seq", "head"),
        P("seq", "head"),
        P("seq", "head"),
        P("head", "seq"),
        P(),
        P("seq", "head"),
        P("seq", "head"),
        P("seq", "head"),
        P("seq", None),
        P(),
    )
    out_specs = P("seq", "head")
    return jax.shard_map(
        per_device, mesh=mesh, in_specs=in_specs, out_specs=out_specs, check_vma=False
    )
```

```python
import functools

import jax
import jax.numpy as jnp
from jax import lax
from jax.experimental import pallas as pl
from jax.experimental.pallas import tpu as pltpu
from jax.sharding import PartitionSpec as P

D = 4096
HEADS = 32
KV_HEADS = 8
HD = 128
BLOCK = 512
KMAX = 256
GROUP = HEADS // KV_HEADS
N_Z = 8
N_Y = 8
N_X = 4
TAIL = 16
STRIP = D // (N_Z * N_Y)
HALF = N_Y // 2 * STRIP
QW = GROUP * HD
KVW = 2 * HD
LOG2E = 1.4426950408889634
SCALE = HD**-0.5 * LOG2E
NEG = -1e30
VMEM_LIMIT = 48 * 1024 * 1024

Z_GROUPS = [[z * N_Y + y for z in range(N_Z)] for y in range(N_Y)]
X_GROUPS = [[2 * x + c for x in range(N_X)] for c in range(2)]
CORE_SWAP = [(i, i ^ 1) for i in range(2 * N_X)]
SIBLING_SWAP = [(i, i ^ 1) for i in range(N_Z * N_Y)]
PARITY_GROUPS = [[z * N_Y + 2 * p + q for p in range(N_Y // 2)] for z in range(N_Z) for q in range(2)]


def params():
    return pltpu.CompilerParams(vmem_limit_bytes=VMEM_LIMIT)


def dot(a, b):
    return jnp.dot(a, b, preferred_element_type=jnp.float32)


def dot_t(a, b):
    return lax.dot_general(a, b, (((1,), (1,)), ((), ())), preferred_element_type=jnp.float32)


def with_ones(values):
    return jnp.concatenate([values, jnp.ones_like(values)], axis=1)


def attend(scores, values):
    top = jnp.max(scores, axis=1, keepdims=True)
    unnormed = jnp.exp2(scores - top).astype(jnp.bfloat16)
    sums = dot(unnormed, values)
    return sums[:, :HD] / sums[:, HD : HD + 1]


def lower_kernel(
    place_ref, index_ref, q_ref, k_ref, v_ref, hidden_ref, gain_ref, inverse_ref, out_ref, hid_ref
):
    index = index_ref[...]
    column = lax.broadcasted_iota(jnp.int32, (KMAX, BLOCK), 1)
    pick = (column == index).astype(jnp.bfloat16)
    causal = column <= index
    queries = dot(pick, q_ref[...]).astype(jnp.bfloat16)
    keys = k_ref[...]
    values = with_ones(v_ref[...])
    for g in range(GROUP):
        cols = slice(g * HD, (g + 1) * HD)
        scores = jnp.where(causal, dot_t(queries[:, cols], keys) * SCALE, NEG)
        out_ref[:, cols] = attend(scores, values).astype(jnp.bfloat16)
    kept = dot(pick, hidden_ref[...]).astype(jnp.bfloat16)
    row = lax.broadcasted_iota(jnp.int32, (QW, HALF), 0)
    col = lax.broadcasted_iota(jnp.int32, (QW, HALF), 1)
    for ref, parity in ((hid_ref, place_ref[1]), (out_ref.at[:, QW:], 1 - place_ref[1])):
        source = (col // STRIP) * (2 * STRIP) + parity * STRIP + col % STRIP
        ref[...] = dot(kept, (row == source).astype(jnp.bfloat16)).astype(jnp.bfloat16)


def lower(place, index, queries, keys, values, hidden, gain, inverse):
    return pl.pallas_call(
        lower_kernel,
        in_specs=[pl.BlockSpec(memory_space=pltpu.SMEM)]
        + [pl.BlockSpec(memory_space=pltpu.VMEM)] * 5
        + [pl.BlockSpec(memory_space=pl.ANY)] * 2,
        out_shape=[
            jax.ShapeDtypeStruct((KMAX, QW + HALF), jnp.bfloat16),
            jax.ShapeDtypeStruct((KMAX, HALF), jnp.bfloat16),
        ],
        compiler_params=params(),
        name="lower",
    )(place, index, queries, keys, values, hidden, gain, inverse)


def project_kernel(other, place_ref, own_ref, pair_ref, weight_ref, out_ref):
    core = 1 - place_ref[0] if other else place_ref[0]
    own = own_ref[:, :QW]
    pair = pair_ref[:, :QW]
    for x in range(N_X):
        weights = weight_ref[2 * x + core]
        out_ref[x, :KMAX] = dot_t(own, weights).astype(out_ref.dtype)
        out_ref[x, KMAX:] = dot_t(pair, weights).astype(out_ref.dtype)


def project(place, kept, kept_pair, weights, other):
    return pl.pallas_call(
        functools.partial(project_kernel, other),
        in_specs=[pl.BlockSpec(memory_space=pltpu.SMEM)] + [pl.BlockSpec(memory_space=pltpu.VMEM)] * 3,
        out_specs=pl.BlockSpec(memory_space=pltpu.VMEM),
        out_shape=jax.ShapeDtypeStruct(
            (N_X, 2 * KMAX, HALF), jnp.bfloat16 if other else jnp.float32
        ),
        compiler_params=params(),
        cost_estimate=pl.CostEstimate(flops=2**30 // 2, bytes_accessed=2**20, transcendentals=0),
        name="project_other" if other else "project_mine",
    )(place, kept, kept_pair, weights)


def state_kernel(place_ref, parts_ref, hid_ref, pair_ref, gain_ref, out_ref):
    gain = gain_ref[place_ref[4]]
    for half, hid in enumerate((hid_ref, pair_ref.at[:, QW:])):
        rows = slice(half * KMAX, (half + 1) * KMAX)
        total = hid[...].astype(jnp.float32)
        for x in range(N_X):
            total += parts_ref[x, rows].astype(jnp.float32)
        state = total.astype(jnp.bfloat16).astype(jnp.float32)
        scaled = (state * gain).astype(jnp.bfloat16)
        for x in range(N_X):
            out_ref[x, rows] = scaled


def add_up(place, parts, hid, kept_pair, gain):
    return pl.pallas_call(
        state_kernel,
        in_specs=[pl.BlockSpec(memory_space=pltpu.SMEM)] + [pl.BlockSpec(memory_space=pltpu.VMEM)] * 4,
        out_shape=jax.ShapeDtypeStruct((N_X, 2 * KMAX, HALF), jnp.bfloat16),
        compiler_params=params(),
        name="state",
    )(place, parts, hid, kept_pair, gain)


def by_core(core):
    return [2 * x + core for x in range(N_X)] + [2 * x + 1 - core for x in range(N_X)]


OWN = slice(0, KMAX)
PAIR = slice(KMAX, 2 * KMAX)


def contract(rows, mine_ref, other_ref, weights):
    state = [ref[x, rows] for ref in (mine_ref, other_ref) for x in range(N_X)]
    return dot(jnp.concatenate(state, axis=1), weights)


def kv_kernel(place_ref, mine_ref, other_ref, weight_ref, keep_ref, send_ref, kv_ref, first_ref, sems):
    heads = by_core(place_ref[0])
    copies = []
    for cols, buffer in ((pl.ds(QW, KVW), kv_ref), (pl.ds(0, HD), first_ref)):
        for i, head in enumerate(heads):
            source = weight_ref.at[head, :, cols]
            copies.append(pltpu.make_async_copy(source, buffer.at[i], sems.at[len(copies)]))
            copies[-1].start()
    for copy in copies[: 2 * N_X]:
        copy.wait()
    weights = kv_ref[...].reshape(2 * N_X * HALF, KVW)
    for half, rows in enumerate((OWN, PAIR)):
        sums = contract(rows, mine_ref, other_ref, weights)
        keep_ref[rows] = sums
        send_ref[:, (1 - half) * KVW : (2 - half) * KVW] = sums.astype(jnp.bfloat16)
    for copy in copies[2 * N_X :]:
        copy.wait()
    sums = contract(PAIR, mine_ref, other_ref, first_ref[...].reshape(2 * N_X * HALF, HD))
    send_ref[:, 2 * KVW :] = sums.astype(jnp.bfloat16)


def project_kv(place, mine, other, weights):
    return pl.pallas_call(
        kv_kernel,
        in_specs=[
            pl.BlockSpec(memory_space=pltpu.SMEM),
            pl.BlockSpec(memory_space=pltpu.VMEM),
            pl.BlockSpec(memory_space=pltpu.VMEM),
            pl.BlockSpec(memory_space=pl.ANY),
        ],
        out_specs=[pl.BlockSpec(memory_space=pltpu.VMEM)] * 2,
        out_shape=[
            jax.ShapeDtypeStruct((2 * KMAX, KVW), jnp.float32),
            jax.ShapeDtypeStruct((KMAX, 2 * KVW + HD), jnp.bfloat16),
        ],
        scratch_shapes=[
            pltpu.VMEM((2 * N_X, HALF, KVW), jnp.bfloat16),
            pltpu.VMEM((2 * N_X, HALF, HD), jnp.bfloat16),
            pltpu.SemaphoreType.DMA((4 * N_X,)),
        ],
        compiler_params=pltpu.CompilerParams(vmem_limit_bytes=50 * 1024 * 1024),
        name="project_kv",
    )(place, mine, other, weights)


def sibling_kernel(
    place_ref, mine_ref, other_ref, weight_ref, inverse_ref, first_ref, square_ref, send_ref
):
    heads = by_core(place_ref[0])
    weights = jnp.concatenate([weight_ref[head, :, HD:QW] for head in heads], axis=0)
    sums = contract(PAIR, mine_ref, other_ref, weights)
    send_ref[:KMAX] = sums.astype(jnp.bfloat16)
    squares = jnp.zeros((2 * KMAX, HD), jnp.float32)
    for i, head in enumerate(heads):
        scaled = (mine_ref if i < N_X else other_ref)[i % N_X].astype(jnp.float32)
        square = scaled * scaled * inverse_ref[head]
        squares += square[:, :HD] + square[:, HD:]
    total = jnp.sum(squares, axis=1, keepdims=True)
    square_ref[...] = jnp.broadcast_to(total, square_ref.shape)
    across = lax.dot_general(
        jnp.ones((TAIL, HD), jnp.float32),
        squares,
        (((1,), (1,)), ((), ())),
        precision=lax.Precision.HIGHEST,
        preferred_element_type=jnp.float32,
    )
    high = across.astype(jnp.bfloat16).astype(jnp.float32)
    low = across - high
    row = lax.broadcasted_iota(jnp.int32, (TAIL, KMAX), 0)
    tail = jnp.where(
        row == 0,
        high[:, PAIR],
        jnp.where(row == 1, low[:, PAIR], jnp.where(row == 2, high[:, OWN], low[:, OWN])),
    )
    send_ref[KMAX:] = jnp.concatenate([tail, tail[:, :HD]], axis=1).astype(jnp.bfloat16)


def project_sibling(place, mine, other, weights, inverse, first):
    return pl.pallas_call(
        sibling_kernel,
        in_specs=[pl.BlockSpec(memory_space=pltpu.SMEM)]
        + [pl.BlockSpec(memory_space=pltpu.VMEM)] * 4
        + [pl.BlockSpec(memory_space=pl.ANY)],
        out_specs=[pl.BlockSpec(memory_space=pltpu.VMEM)] * 2,
        out_shape=[
            jax.ShapeDtypeStruct((2 * KMAX, HD), jnp.float32),
            jax.ShapeDtypeStruct((KMAX + TAIL, QW - HD), jnp.bfloat16),
        ],
        compiler_params=params(),
        cost_estimate=pl.CostEstimate(flops=2**29, bytes_accessed=2**22, transcendentals=0),
        name="project_sibling",
    )(place, mine, other, weights, inverse, first)


def q_kernel(place_ref, mine_ref, other_ref, weight_ref, first_ref, out_ref):
    heads = by_core(place_ref[0])
    weights = jnp.concatenate([weight_ref[head, :, :QW] for head in heads], axis=0)
    out_ref[...] = contract(OWN, mine_ref, other_ref, weights)


def project_q(place, mine, other, weights, first):
    return pl.pallas_call(
        q_kernel,
        in_specs=[pl.BlockSpec(memory_space=pltpu.SMEM)]
        + [pl.BlockSpec(memory_space=pltpu.VMEM)] * 3
        + [pl.BlockSpec(memory_space=pl.ANY)],
        out_specs=pl.BlockSpec(memory_space=pltpu.VMEM),
        out_shape=jax.ShapeDtypeStruct((KMAX, QW), jnp.float32),
        compiler_params=params(),
        cost_estimate=pl.CostEstimate(flops=2**29, bytes_accessed=2**22, transcendentals=0),
        name="project_q",
    )(place, mine, other, weights, first)


def upper_kernel(place_ref, q_ref, kv_ref, square_ref, got_q_ref, got_kv_ref, out_ref):
    parity = place_ref[1]
    own_count = place_ref[2]
    left_count = place_ref[3]
    tail = got_q_ref[KMAX:, :KMAX].astype(jnp.float32)
    same = lax.broadcasted_iota(jnp.int32, (KMAX, KMAX), 0) == lax.broadcasted_iota(
        jnp.int32, (KMAX, KMAX), 1
    )

    def down(across):
        return jnp.sum(jnp.where(same, across, 0.0), axis=1, keepdims=True)

    own_sum = square_ref[:KMAX, :1] + down(tail[0:1] + tail[1:2])
    pair_sum = square_ref[KMAX:, :1] + down(tail[2:3] + tail[3:4])
    own_inv = lax.rsqrt(own_sum / D + 1e-05)
    pair_inv = lax.rsqrt(pair_sum / D + 1e-05)
    got = jnp.concatenate([got_kv_ref[:, 2 * KVW :], got_q_ref[:KMAX]], axis=1)
    queries = ((q_ref[...] + got.astype(jnp.float32)) * own_inv).astype(jnp.bfloat16)
    own = (kv_ref[:KMAX] + got_kv_ref[:, :KVW].astype(jnp.float32)) * own_inv
    own = own.astype(jnp.bfloat16)
    pair = (kv_ref[KMAX:] + got_kv_ref[:, KVW : 2 * KVW].astype(jnp.float32)) * pair_inv
    pair = pair.astype(jnp.bfloat16)
    keys = jnp.concatenate([pair[:, :HD], own[:, :HD]], axis=0)
    values = with_ones(jnp.concatenate([pair[:, HD:], own[:, HD:]], axis=0))
    row = lax.broadcasted_iota(jnp.int32, (KMAX, 2 * KMAX), 0)
    col = lax.broadcasted_iota(jnp.int32, (KMAX, 2 * KMAX), 1)
    from_left = col < left_count * parity
    from_own = (col >= KMAX) & (col - KMAX <= row) & (col - KMAX < own_count)
    allowed = from_left | from_own
    valid = lax.broadcasted_iota(jnp.int32, (KMAX, HD), 0) < own_count
    for g in range(GROUP):
        cols = slice(g * HD, (g + 1) * HD)
        scores = jnp.where(allowed, dot_t(queries[:, cols], keys) * SCALE, NEG)
        out_ref[:, cols] = jnp.where(valid, attend(scores, values), 0.0).astype(jnp.bfloat16)


def upper(place, q, kv, squares, got_q, got_kv):
    return pl.pallas_call(
        upper_kernel,
        in_specs=[pl.BlockSpec(memory_space=pltpu.SMEM)] + [pl.BlockSpec(memory_space=pltpu.VMEM)] * 5,
        out_shape=jax.ShapeDtypeStruct((KMAX, QW), jnp.bfloat16),
        compiler_params=params(),
        name="upper",
    )(place, q, kv, squares, got_q, got_kv)


def gather_head(x):
    mine = lax.all_to_all(x, "head", 0, 0, axis_index_groups=X_GROUPS, tiled=True)
    return mine, lax.ppermute(mine, "head", CORE_SWAP)


def per_device(
    hidden,
    queries,
    keys_low,
    values_low,
    out_weight,
    norm_gain,
    query_weight,
    key_weight,
    value_weight,
    keep_index,
    keep_count,
):
    seq = lax.axis_index("seq")
    parity = seq % 2
    head = lax.axis_index("head")
    core = head % 2
    own_count = lax.dynamic_index_in_dim(keep_count, seq, keepdims=False)
    left_count = lax.dynamic_index_in_dim(keep_count, jnp.maximum(seq - 1, 0), keepdims=False)
    place = jnp.stack([core, parity, own_count, left_count, head]).astype(jnp.int32)

    shard = out_weight.T
    shards = lax.all_to_all(
        jnp.broadcast_to(shard, (N_Y // 2,) + shard.shape),
        "seq",
        0,
        0,
        axis_index_groups=PARITY_GROUPS,
        tiled=True,
    )
    out_weights = lax.all_gather(
        shards.reshape(HALF, QW), "seq", axis=0, axis_index_groups=Z_GROUPS
    )

    gain = lax.dynamic_index_in_dim(
        norm_gain.reshape(8, N_Y // 2, 2, STRIP), parity, axis=2, keepdims=False
    ).reshape(8, 1, HALF)
    inverse = 1.0 / (gain * gain)
    index = keep_index.reshape(KMAX, 1)
    kept, hid = lower(place, index, queries, keys_low, values_low, hidden, gain, inverse)
    kept_pair = lax.ppermute(kept, "seq", SIBLING_SWAP)

    shard = jnp.concatenate([query_weight, key_weight, value_weight], axis=1)
    shards = lax.all_gather(shard, "seq", axis=0, axis_index_groups=PARITY_GROUPS, tiled=True)
    qkv_weights = lax.all_gather(shards, "seq", axis=0, axis_index_groups=Z_GROUPS)

    send = project(place, kept, kept_pair, out_weights, True)
    got = lax.ppermute(send, "head", CORE_SWAP)
    keep = project(place, kept, kept_pair, out_weights, False)
    parts = (keep + got.astype(jnp.float32)).astype(jnp.bfloat16)
    parts = lax.all_to_all(parts, "head", 0, 0, axis_index_groups=X_GROUPS, tiled=True)
    mine, other = gather_head(add_up(place, parts, hid, kept_pair, gain))

    kv, send = project_kv(place, mine, other, qkv_weights)
    got_kv = lax.ppermute(send, "seq", SIBLING_SWAP)
    squares, send = project_sibling(place, mine, other, qkv_weights, inverse, kv)
    got_q = lax.ppermute(send, "seq", SIBLING_SWAP)
    q = project_q(place, mine, other, qkv_weights, send)
    return upper(place, q, kv, squares, got_q, got_kv)


def solution(mesh):
    in_specs = (
        P("seq", "head"),
        P("seq", "head"),
        P("seq", "head"),
        P("seq", "head"),
        P("head", "seq"),
        P(),
        P("seq", "head"),
        P("seq", "head"),
        P("seq", "head"),
        P("seq", None),
        P(),
    )
    out_specs = P("seq", "head")
    return jax.shard_map(
        per_device, mesh=mesh, in_specs=in_specs, out_specs=out_specs, check_vma=False
    )
```

```python
import functools

import jax
import jax.numpy as jnp
from jax import lax
from jax.experimental import pallas as pl
from jax.experimental.pallas import tpu as pltpu
from jax.sharding import PartitionSpec as P

D = 4096
HEADS = 32
KV_HEADS = 8
HD = 128
BLOCK = 512
KMAX = 256
GROUP = HEADS // KV_HEADS
N_Z = 8
N_Y = 8
N_X = 4
TAIL = 16
STRIP = D // (N_Z * N_Y)
HALF = N_Y // 2 * STRIP
QW = GROUP * HD
KVW = 2 * HD
LOG2E = 1.4426950408889634
SCALE = HD**-0.5 * LOG2E
NEG = -1e30
VMEM_LIMIT = 48 * 1024 * 1024

Z_GROUPS = [[z * N_Y + y for z in range(N_Z)] for y in range(N_Y)]
X_GROUPS = [[2 * x + c for x in range(N_X)] for c in range(2)]
CORE_SWAP = [(i, i ^ 1) for i in range(2 * N_X)]
SIBLING_SWAP = [(i, i ^ 1) for i in range(N_Z * N_Y)]
PARITY_GROUPS = [[z * N_Y + 2 * p + q for p in range(N_Y // 2)] for z in range(N_Z) for q in range(2)]


def params():
    return pltpu.CompilerParams(vmem_limit_bytes=VMEM_LIMIT)


def dot(a, b):
    return jnp.dot(a, b, preferred_element_type=jnp.float32)


def dot_t(a, b):
    return lax.dot_general(a, b, (((1,), (1,)), ((), ())), preferred_element_type=jnp.float32)


def with_ones(values):
    return jnp.concatenate([values, jnp.ones_like(values)], axis=1)


def attend(scores, values):
    top = jnp.max(scores, axis=1, keepdims=True)
    unnormed = jnp.exp2(scores - top).astype(jnp.bfloat16)
    sums = dot(unnormed, values)
    return sums[:, :HD] / sums[:, HD : HD + 1]


def lower_kernel(
    place_ref, index_ref, q_ref, k_ref, v_ref, hidden_ref, gain_ref, inverse_ref, out_ref, hid_ref
):
    index = index_ref[...]
    column = lax.broadcasted_iota(jnp.int32, (KMAX, BLOCK), 1)
    pick = (column == index).astype(jnp.bfloat16)
    causal = column <= index
    queries = dot(pick, q_ref[...]).astype(jnp.bfloat16)
    keys = k_ref[...]
    values = with_ones(v_ref[...])
    for g in range(GROUP):
        cols = slice(g * HD, (g + 1) * HD)
        scores = jnp.where(causal, dot_t(queries[:, cols], keys) * SCALE, NEG)
        out_ref[:, cols] = attend(scores, values).astype(jnp.bfloat16)
    kept = dot(pick, hidden_ref[...]).astype(jnp.bfloat16)
    row = lax.broadcasted_iota(jnp.int32, (QW, HALF), 0)
    col = lax.broadcasted_iota(jnp.int32, (QW, HALF), 1)
    for ref, parity in ((hid_ref, place_ref[1]), (out_ref.at[:, QW:], 1 - place_ref[1])):
        source = (col // STRIP) * (2 * STRIP) + parity * STRIP + col % STRIP
        ref[...] = dot(kept, (row == source).astype(jnp.bfloat16)).astype(jnp.bfloat16)


def lower(place, index, queries, keys, values, hidden, gain, inverse):
    return pl.pallas_call(
        lower_kernel,
        in_specs=[pl.BlockSpec(memory_space=pltpu.SMEM)]
        + [pl.BlockSpec(memory_space=pltpu.VMEM)] * 5
        + [pl.BlockSpec(memory_space=pl.ANY)] * 2,
        out_shape=[
            jax.ShapeDtypeStruct((KMAX, QW + HALF), jnp.bfloat16),
            jax.ShapeDtypeStruct((KMAX, HALF), jnp.bfloat16),
        ],
        compiler_params=params(),
        name="lower",
    )(place, index, queries, keys, values, hidden, gain, inverse)


def project_kernel(other, place_ref, own_ref, pair_ref, weight_ref, out_ref):
    core = 1 - place_ref[0] if other else place_ref[0]
    own = own_ref[:, :QW]
    pair = pair_ref[:, :QW]
    for x in range(N_X):
        weights = weight_ref[2 * x + core]
        out_ref[x, :KMAX] = dot_t(own, weights).astype(out_ref.dtype)
        out_ref[x, KMAX:] = dot_t(pair, weights).astype(out_ref.dtype)


def project(place, kept, kept_pair, weights, other):
    return pl.pallas_call(
        functools.partial(project_kernel, other),
        in_specs=[pl.BlockSpec(memory_space=pltpu.SMEM)] + [pl.BlockSpec(memory_space=pltpu.VMEM)] * 3,
        out_specs=pl.BlockSpec(memory_space=pltpu.VMEM),
        out_shape=jax.ShapeDtypeStruct(
            (N_X, 2 * KMAX, HALF), jnp.bfloat16 if other else jnp.float32
        ),
        compiler_params=params(),
        cost_estimate=pl.CostEstimate(flops=2**30 // 2, bytes_accessed=2**20, transcendentals=0),
        name="project_other" if other else "project_mine",
    )(place, kept, kept_pair, weights)


def state_kernel(place_ref, parts_ref, hid_ref, pair_ref, gain_ref, out_ref):
    gain = gain_ref[place_ref[4]]
    for half, hid in enumerate((hid_ref, pair_ref.at[:, QW:])):
        rows = slice(half * KMAX, (half + 1) * KMAX)
        total = hid[...].astype(jnp.float32)
        for x in range(N_X):
            total += parts_ref[x, rows].astype(jnp.float32)
        state = total.astype(jnp.bfloat16).astype(jnp.float32)
        scaled = (state * gain).astype(jnp.bfloat16)
        for x in range(N_X):
            out_ref[x, rows] = scaled


def add_up(place, parts, hid, kept_pair, gain):
    return pl.pallas_call(
        state_kernel,
        in_specs=[pl.BlockSpec(memory_space=pltpu.SMEM)] + [pl.BlockSpec(memory_space=pltpu.VMEM)] * 4,
        out_shape=jax.ShapeDtypeStruct((N_X, 2 * KMAX, HALF), jnp.bfloat16),
        compiler_params=params(),
        name="state",
    )(place, parts, hid, kept_pair, gain)


def by_core(core):
    return [2 * x + core for x in range(N_X)] + [2 * x + 1 - core for x in range(N_X)]


OWN = slice(0, KMAX)
PAIR = slice(KMAX, 2 * KMAX)


def contract(rows, mine_ref, other_ref, weights):
    state = [ref[x, rows] for ref in (mine_ref, other_ref) for x in range(N_X)]
    return dot(jnp.concatenate(state, axis=1), weights)


def kv_kernel(place_ref, mine_ref, other_ref, weight_ref, keep_ref, send_ref, kv_ref, sems):
    heads = by_core(place_ref[0])
    copies = [
        pltpu.make_async_copy(weight_ref.at[head, :, pl.ds(QW, KVW)], kv_ref.at[i], sems.at[i])
        for i, head in enumerate(heads)
    ]
    for copy in copies:
        copy.start()
    for copy in copies:
        copy.wait()
    weights = kv_ref[...].reshape(2 * N_X * HALF, KVW)
    for half, rows in enumerate((OWN, PAIR)):
        sums = contract(rows, mine_ref, other_ref, weights)
        keep_ref[rows] = sums
        send_ref[:, (1 - half) * KVW : (2 - half) * KVW] = sums.astype(jnp.bfloat16)


def project_kv(place, mine, other, weights):
    return pl.pallas_call(
        kv_kernel,
        in_specs=[
            pl.BlockSpec(memory_space=pltpu.SMEM),
            pl.BlockSpec(memory_space=pltpu.VMEM),
            pl.BlockSpec(memory_space=pltpu.VMEM),
            pl.BlockSpec(memory_space=pl.ANY),
        ],
        out_specs=[pl.BlockSpec(memory_space=pltpu.VMEM)] * 2,
        out_shape=[
            jax.ShapeDtypeStruct((2 * KMAX, KVW), jnp.float32),
            jax.ShapeDtypeStruct((KMAX, 2 * KVW), jnp.bfloat16),
        ],
        scratch_shapes=[
            pltpu.VMEM((2 * N_X, HALF, KVW), jnp.bfloat16),
            pltpu.SemaphoreType.DMA((2 * N_X,)),
        ],
        compiler_params=pltpu.CompilerParams(vmem_limit_bytes=50 * 1024 * 1024),
        name="project_kv",
    )(place, mine, other, weights)


def sibling_kernel(
    place_ref, mine_ref, other_ref, weight_ref, inverse_ref, first_ref, square_ref, send_ref, last_ref
):
    heads = by_core(place_ref[0])
    weights = jnp.concatenate([weight_ref[head, :, :QW] for head in heads], axis=0)
    sums = contract(PAIR, mine_ref, other_ref, weights)
    send_ref[...] = sums[:, :KMAX].astype(jnp.bfloat16)
    last_ref[:KMAX] = sums[:, KMAX:].astype(jnp.bfloat16)
    squares = jnp.zeros((2 * KMAX, HD), jnp.float32)
    for i, head in enumerate(heads):
        scaled = (mine_ref if i < N_X else other_ref)[i % N_X].astype(jnp.float32)
        square = scaled * scaled * inverse_ref[head]
        squares += square[:, :HD] + square[:, HD:]
    total = jnp.sum(squares, axis=1, keepdims=True)
    square_ref[...] = jnp.broadcast_to(total, square_ref.shape)
    across = lax.dot_general(
        jnp.ones((TAIL, HD), jnp.float32),
        squares,
        (((1,), (1,)), ((), ())),
        precision=lax.Precision.HIGHEST,
        preferred_element_type=jnp.float32,
    )
    high = across.astype(jnp.bfloat16).astype(jnp.float32)
    low = across - high
    row = lax.broadcasted_iota(jnp.int32, (TAIL, KMAX), 0)
    tail = jnp.where(
        row == 0,
        high[:, PAIR],
        jnp.where(row == 1, low[:, PAIR], jnp.where(row == 2, high[:, OWN], low[:, OWN])),
    )
    last_ref[KMAX:] = tail.astype(jnp.bfloat16)


def project_sibling(place, mine, other, weights, inverse, first):
    return pl.pallas_call(
        sibling_kernel,
        in_specs=[pl.BlockSpec(memory_space=pltpu.SMEM)]
        + [pl.BlockSpec(memory_space=pltpu.VMEM)] * 4
        + [pl.BlockSpec(memory_space=pl.ANY)],
        out_specs=[pl.BlockSpec(memory_space=pltpu.VMEM)] * 3,
        out_shape=[
            jax.ShapeDtypeStruct((2 * KMAX, HD), jnp.float32),
            jax.ShapeDtypeStruct((KMAX, KMAX), jnp.bfloat16),
            jax.ShapeDtypeStruct((KMAX + TAIL, KMAX), jnp.bfloat16),
        ],
        compiler_params=params(),
        cost_estimate=pl.CostEstimate(flops=2**29, bytes_accessed=2**22, transcendentals=0),
        name="project_sibling",
    )(place, mine, other, weights, inverse, first)


def q_kernel(place_ref, mine_ref, other_ref, weight_ref, first_ref, out_ref):
    heads = by_core(place_ref[0])
    weights = jnp.concatenate([weight_ref[head, :, :QW] for head in heads], axis=0)
    out_ref[...] = contract(OWN, mine_ref, other_ref, weights)


def project_q(place, mine, other, weights, first):
    return pl.pallas_call(
        q_kernel,
        in_specs=[pl.BlockSpec(memory_space=pltpu.SMEM)]
        + [pl.BlockSpec(memory_space=pltpu.VMEM)] * 3
        + [pl.BlockSpec(memory_space=pl.ANY)],
        out_specs=pl.BlockSpec(memory_space=pltpu.VMEM),
        out_shape=jax.ShapeDtypeStruct((KMAX, QW), jnp.float32),
        compiler_params=params(),
        cost_estimate=pl.CostEstimate(flops=2**29, bytes_accessed=2**22, transcendentals=0),
        name="project_q",
    )(place, mine, other, weights, first)


def upper_kernel(place_ref, q_ref, kv_ref, square_ref, got_q_ref, got_last_ref, got_kv_ref, out_ref):
    parity = place_ref[1]
    own_count = place_ref[2]
    left_count = place_ref[3]
    tail = got_last_ref[KMAX:].astype(jnp.float32)
    same = lax.broadcasted_iota(jnp.int32, (KMAX, KMAX), 0) == lax.broadcasted_iota(
        jnp.int32, (KMAX, KMAX), 1
    )

    def down(across):
        return jnp.sum(jnp.where(same, across, 0.0), axis=1, keepdims=True)

    own_sum = square_ref[:KMAX, :1] + down(tail[0:1] + tail[1:2])
    pair_sum = square_ref[KMAX:, :1] + down(tail[2:3] + tail[3:4])
    own_inv = lax.rsqrt(own_sum / D + 1e-05)
    pair_inv = lax.rsqrt(pair_sum / D + 1e-05)
    got = jnp.concatenate([got_q_ref[...], got_last_ref[:KMAX]], axis=1)
    queries = ((q_ref[...] + got.astype(jnp.float32)) * own_inv).astype(jnp.bfloat16)
    own = (kv_ref[:KMAX] + got_kv_ref[:, :KVW].astype(jnp.float32)) * own_inv
    own = own.astype(jnp.bfloat16)
    pair = (kv_ref[KMAX:] + got_kv_ref[:, KVW : 2 * KVW].astype(jnp.float32)) * pair_inv
    pair = pair.astype(jnp.bfloat16)
    keys = jnp.concatenate([pair[:, :HD], own[:, :HD]], axis=0)
    values = with_ones(jnp.concatenate([pair[:, HD:], own[:, HD:]], axis=0))
    row = lax.broadcasted_iota(jnp.int32, (KMAX, 2 * KMAX), 0)
    col = lax.broadcasted_iota(jnp.int32, (KMAX, 2 * KMAX), 1)
    from_left = col < left_count * parity
    from_own = (col >= KMAX) & (col - KMAX <= row) & (col - KMAX < own_count)
    allowed = from_left | from_own
    valid = lax.broadcasted_iota(jnp.int32, (KMAX, HD), 0) < own_count
    for g in range(GROUP):
        cols = slice(g * HD, (g + 1) * HD)
        scores = jnp.where(allowed, dot_t(queries[:, cols], keys) * SCALE, NEG)
        out_ref[:, cols] = jnp.where(valid, attend(scores, values), 0.0).astype(jnp.bfloat16)


def upper(place, q, kv, squares, got_q, got_last, got_kv):
    return pl.pallas_call(
        upper_kernel,
        in_specs=[pl.BlockSpec(memory_space=pltpu.SMEM)] + [pl.BlockSpec(memory_space=pltpu.VMEM)] * 6,
        out_shape=jax.ShapeDtypeStruct((KMAX, QW), jnp.bfloat16),
        compiler_params=params(),
        name="upper",
    )(place, q, kv, squares, got_q, got_last, got_kv)


def gather_head(x):
    mine = lax.all_to_all(x, "head", 0, 0, axis_index_groups=X_GROUPS, tiled=True)
    return mine, lax.ppermute(mine, "head", CORE_SWAP)


def per_device(
    hidden,
    queries,
    keys_low,
    values_low,
    out_weight,
    norm_gain,
    query_weight,
    key_weight,
    value_weight,
    keep_index,
    keep_count,
):
    seq = lax.axis_index("seq")
    parity = seq % 2
    head = lax.axis_index("head")
    core = head % 2
    own_count = lax.dynamic_index_in_dim(keep_count, seq, keepdims=False)
    left_count = lax.dynamic_index_in_dim(keep_count, jnp.maximum(seq - 1, 0), keepdims=False)
    place = jnp.stack([core, parity, own_count, left_count, head]).astype(jnp.int32)

    shard = out_weight.T
    shards = lax.all_to_all(
        jnp.broadcast_to(shard, (N_Y // 2,) + shard.shape),
        "seq",
        0,
        0,
        axis_index_groups=PARITY_GROUPS,
        tiled=True,
    )
    out_weights = lax.all_gather(
        shards.reshape(HALF, QW), "seq", axis=0, axis_index_groups=Z_GROUPS
    )

    gain = lax.dynamic_index_in_dim(
        norm_gain.reshape(8, N_Y // 2, 2, STRIP), parity, axis=2, keepdims=False
    ).reshape(8, 1, HALF)
    inverse = 1.0 / (gain * gain)
    index = keep_index.reshape(KMAX, 1)
    kept, hid = lower(place, index, queries, keys_low, values_low, hidden, gain, inverse)
    kept_pair = lax.ppermute(kept, "seq", SIBLING_SWAP)

    shard = jnp.concatenate([query_weight, key_weight, value_weight], axis=1)
    shards = lax.all_gather(shard, "seq", axis=0, axis_index_groups=PARITY_GROUPS, tiled=True)
    qkv_weights = lax.all_gather(shards, "seq", axis=0, axis_index_groups=Z_GROUPS)

    send = project(place, kept, kept_pair, out_weights, True)
    got = lax.ppermute(send, "head", CORE_SWAP)
    keep = project(place, kept, kept_pair, out_weights, False)
    parts = (keep + got.astype(jnp.float32)).astype(jnp.bfloat16)
    parts = lax.all_to_all(parts, "head", 0, 0, axis_index_groups=X_GROUPS, tiled=True)
    mine, other = gather_head(add_up(place, parts, hid, kept_pair, gain))

    kv, send = project_kv(place, mine, other, qkv_weights)
    got_kv = lax.ppermute(send, "seq", SIBLING_SWAP)
    squares, send, last = project_sibling(place, mine, other, qkv_weights, inverse, kv)
    got_q = lax.ppermute(send, "seq", SIBLING_SWAP)
    got_last = lax.ppermute(last, "seq", SIBLING_SWAP)
    q = project_q(place, mine, other, qkv_weights, send)
    return upper(place, q, kv, squares, got_q, got_last, got_kv)


def solution(mesh):
    in_specs = (
        P("seq", "head"),
        P("seq", "head"),
        P("seq", "head"),
        P("seq", "head"),
        P("head", "seq"),
        P(),
        P("seq", "head"),
        P("seq", "head"),
        P("seq", "head"),
        P("seq", None),
        P(),
    )
    out_specs = P("seq", "head")
    return jax.shard_map(
        per_device, mesh=mesh, in_specs=in_specs, out_specs=out_specs, check_vma=False
    )
```

```python
import functools

import jax
import jax.numpy as jnp
from jax import lax
from jax.experimental import pallas as pl
from jax.experimental.pallas import tpu as pltpu
from jax.sharding import PartitionSpec as P

D = 4096
HEADS = 32
KV_HEADS = 8
HD = 128
BLOCK = 512
KMAX = 256
GROUP = HEADS // KV_HEADS
N_Z = 8
N_Y = 8
N_X = 4
TAIL = 16
STRIP = D // (N_Z * N_Y)
HALF = N_Y // 2 * STRIP
QW = GROUP * HD
KVW = 2 * HD
LOG2E = 1.4426950408889634
SCALE = HD**-0.5 * LOG2E
NEG = -1e30
VMEM_LIMIT = 48 * 1024 * 1024

Z_GROUPS = [[z * N_Y + y for z in range(N_Z)] for y in range(N_Y)]
X_GROUPS = [[2 * x + c for x in range(N_X)] for c in range(2)]
CORE_SWAP = [(i, i ^ 1) for i in range(2 * N_X)]
SIBLING_SWAP = [(i, i ^ 1) for i in range(N_Z * N_Y)]
PARITY_GROUPS = [[z * N_Y + 2 * p + q for p in range(N_Y // 2)] for z in range(N_Z) for q in range(2)]


def params():
    return pltpu.CompilerParams(vmem_limit_bytes=VMEM_LIMIT)


def dot(a, b):
    return jnp.dot(a, b, preferred_element_type=jnp.float32)


def dot_t(a, b):
    return lax.dot_general(a, b, (((1,), (1,)), ((), ())), preferred_element_type=jnp.float32)


def with_ones(values):
    return jnp.concatenate([values, jnp.ones_like(values)], axis=1)


def attend(scores, values):
    top = jnp.max(scores, axis=1, keepdims=True)
    unnormed = jnp.exp2(scores - top).astype(jnp.bfloat16)
    sums = dot(unnormed, values)
    return sums[:, :HD] / sums[:, HD : HD + 1]


def lower_kernel(
    place_ref, index_ref, q_ref, k_ref, v_ref, hidden_ref, gain_ref, inverse_ref, out_ref, hid_ref
):
    index = index_ref[...]
    column = lax.broadcasted_iota(jnp.int32, (KMAX, BLOCK), 1)
    pick = (column == index).astype(jnp.bfloat16)
    causal = column <= index
    queries = dot(pick, q_ref[...]).astype(jnp.bfloat16)
    keys = k_ref[...]
    values = with_ones(v_ref[...])
    for g in range(GROUP):
        cols = slice(g * HD, (g + 1) * HD)
        scores = jnp.where(causal, dot_t(queries[:, cols], keys) * SCALE, NEG)
        out_ref[:, cols] = attend(scores, values).astype(jnp.bfloat16)
    kept = dot(pick, hidden_ref[...]).astype(jnp.bfloat16)
    row = lax.broadcasted_iota(jnp.int32, (QW, HALF), 0)
    col = lax.broadcasted_iota(jnp.int32, (QW, HALF), 1)
    for ref, parity in ((hid_ref, place_ref[1]), (out_ref.at[:, QW:], 1 - place_ref[1])):
        source = (col // STRIP) * (2 * STRIP) + parity * STRIP + col % STRIP
        ref[...] = dot(kept, (row == source).astype(jnp.bfloat16)).astype(jnp.bfloat16)


def lower(place, index, queries, keys, values, hidden, gain, inverse):
    return pl.pallas_call(
        lower_kernel,
        in_specs=[pl.BlockSpec(memory_space=pltpu.SMEM)]
        + [pl.BlockSpec(memory_space=pltpu.VMEM)] * 5
        + [pl.BlockSpec(memory_space=pl.ANY)] * 2,
        out_shape=[
            jax.ShapeDtypeStruct((KMAX, QW + HALF), jnp.bfloat16),
            jax.ShapeDtypeStruct((KMAX, HALF), jnp.bfloat16),
        ],
        compiler_params=params(),
        name="lower",
    )(place, index, queries, keys, values, hidden, gain, inverse)


def copies_kernel(shard_ref, out_ref):
    shard = shard_ref[...]
    for place in range(N_Y // 2):
        out_ref[place] = shard


def copies_of(shard):
    return pl.pallas_call(
        copies_kernel,
        out_shape=jax.ShapeDtypeStruct((N_Y // 2,) + shard.shape, shard.dtype),
        compiler_params=params(),
        name="copies",
    )(shard)


def project_kernel(other, place_ref, own_ref, pair_ref, weight_ref, out_ref):
    core = 1 - place_ref[0] if other else place_ref[0]
    own = own_ref[:, :QW]
    pair = pair_ref[:, :QW]
    for x in range(N_X):
        weights = weight_ref[2 * x + core]
        out_ref[x, :KMAX] = dot_t(own, weights).astype(out_ref.dtype)
        out_ref[x, KMAX:] = dot_t(pair, weights).astype(out_ref.dtype)


def project(place, kept, kept_pair, weights, other):
    return pl.pallas_call(
        functools.partial(project_kernel, other),
        in_specs=[pl.BlockSpec(memory_space=pltpu.SMEM)] + [pl.BlockSpec(memory_space=pltpu.VMEM)] * 3,
        out_specs=pl.BlockSpec(memory_space=pltpu.VMEM),
        out_shape=jax.ShapeDtypeStruct(
            (N_X, 2 * KMAX, HALF), jnp.bfloat16 if other else jnp.float32
        ),
        compiler_params=params(),
        cost_estimate=pl.CostEstimate(flops=2**30 // 2, bytes_accessed=2**20, transcendentals=0),
        name="project_other" if other else "project_mine",
    )(place, kept, kept_pair, weights)


def state_kernel(place_ref, parts_ref, hid_ref, pair_ref, gain_ref, out_ref):
    gain = gain_ref[place_ref[4]]
    for half, hid in enumerate((hid_ref, pair_ref.at[:, QW:])):
        rows = slice(half * KMAX, (half + 1) * KMAX)
        total = hid[...].astype(jnp.float32)
        for x in range(N_X):
            total += parts_ref[x, rows].astype(jnp.float32)
        state = total.astype(jnp.bfloat16).astype(jnp.float32)
        scaled = (state * gain).astype(jnp.bfloat16)
        for x in range(N_X):
            out_ref[x, rows] = scaled


def add_up(place, parts, hid, kept_pair, gain):
    return pl.pallas_call(
        state_kernel,
        in_specs=[pl.BlockSpec(memory_space=pltpu.SMEM)] + [pl.BlockSpec(memory_space=pltpu.VMEM)] * 4,
        out_shape=jax.ShapeDtypeStruct((N_X, 2 * KMAX, HALF), jnp.bfloat16),
        compiler_params=params(),
        name="state",
    )(place, parts, hid, kept_pair, gain)


def by_core(core):
    return [2 * x + core for x in range(N_X)] + [2 * x + 1 - core for x in range(N_X)]


OWN = slice(0, KMAX)
PAIR = slice(KMAX, 2 * KMAX)


def contract(rows, mine_ref, other_ref, weights):
    state = [ref[x, rows] for ref in (mine_ref, other_ref) for x in range(N_X)]
    return dot(jnp.concatenate(state, axis=1), weights)


def kv_kernel(place_ref, mine_ref, other_ref, weight_ref, keep_ref, send_ref, kv_ref, sems):
    heads = by_core(place_ref[0])
    copies = [
        pltpu.make_async_copy(weight_ref.at[head, :, pl.ds(QW, KVW)], kv_ref.at[i], sems.at[i])
        for i, head in enumerate(heads)
    ]
    for copy in copies:
        copy.start()
    for copy in copies:
        copy.wait()
    weights = kv_ref[...].reshape(2 * N_X * HALF, KVW)
    for at in range(0, 2 * KMAX, HD):
        rows = slice(at, at + HD)
        sums = contract(rows, mine_ref, other_ref, weights)
        keep_ref[rows] = sums
        half, at = divmod(at, KMAX)
        send_ref[at : at + HD, (1 - half) * KVW : (2 - half) * KVW] = sums.astype(jnp.bfloat16)


def project_kv(place, mine, other, weights):
    return pl.pallas_call(
        kv_kernel,
        in_specs=[
            pl.BlockSpec(memory_space=pltpu.SMEM),
            pl.BlockSpec(memory_space=pltpu.VMEM),
            pl.BlockSpec(memory_space=pltpu.VMEM),
            pl.BlockSpec(memory_space=pl.ANY),
        ],
        out_specs=[pl.BlockSpec(memory_space=pltpu.VMEM)] * 2,
        out_shape=[
            jax.ShapeDtypeStruct((2 * KMAX, KVW), jnp.float32),
            jax.ShapeDtypeStruct((KMAX, 2 * KVW), jnp.bfloat16),
        ],
        scratch_shapes=[
            pltpu.VMEM((2 * N_X, HALF, KVW), jnp.bfloat16),
            pltpu.SemaphoreType.DMA((2 * N_X,)),
        ],
        compiler_params=pltpu.CompilerParams(vmem_limit_bytes=50 * 1024 * 1024),
        name="project_kv",
    )(place, mine, other, weights)


def sibling_kernel(
    place_ref, mine_ref, other_ref, weight_ref, inverse_ref, first_ref, square_ref, send_ref, last_ref
):
    heads = by_core(place_ref[0])
    weights = jnp.concatenate([weight_ref[head, :, :QW] for head in heads], axis=0)
    sums = contract(PAIR, mine_ref, other_ref, weights)
    send_ref[...] = sums[:, :KMAX].astype(jnp.bfloat16)
    last_ref[:KMAX] = sums[:, KMAX:].astype(jnp.bfloat16)
    squares = jnp.zeros((2 * KMAX, HD), jnp.float32)
    for i, head in enumerate(heads):
        scaled = (mine_ref if i < N_X else other_ref)[i % N_X].astype(jnp.float32)
        square = scaled * scaled * inverse_ref[head]
        squares += square[:, :HD] + square[:, HD:]
    total = jnp.sum(squares, axis=1, keepdims=True)
    square_ref[...] = jnp.broadcast_to(total, square_ref.shape)
    across = lax.dot_general(
        jnp.ones((TAIL, HD), jnp.float32),
        squares,
        (((1,), (1,)), ((), ())),
        precision=lax.Precision.HIGHEST,
        preferred_element_type=jnp.float32,
    )
    high = across.astype(jnp.bfloat16).astype(jnp.float32)
    low = across - high
    row = lax.broadcasted_iota(jnp.int32, (TAIL, KMAX), 0)
    tail = jnp.where(
        row == 0,
        high[:, PAIR],
        jnp.where(row == 1, low[:, PAIR], jnp.where(row == 2, high[:, OWN], low[:, OWN])),
    )
    last_ref[KMAX:] = tail.astype(jnp.bfloat16)


def project_sibling(place, mine, other, weights, inverse, first):
    return pl.pallas_call(
        sibling_kernel,
        in_specs=[pl.BlockSpec(memory_space=pltpu.SMEM)]
        + [pl.BlockSpec(memory_space=pltpu.VMEM)] * 4
        + [pl.BlockSpec(memory_space=pl.ANY)],
        out_specs=[pl.BlockSpec(memory_space=pltpu.VMEM)] * 3,
        out_shape=[
            jax.ShapeDtypeStruct((2 * KMAX, HD), jnp.float32),
            jax.ShapeDtypeStruct((KMAX, KMAX), jnp.bfloat16),
            jax.ShapeDtypeStruct((KMAX + TAIL, KMAX), jnp.bfloat16),
        ],
        compiler_params=params(),
        cost_estimate=pl.CostEstimate(flops=2**29, bytes_accessed=2**22, transcendentals=0),
        name="project_sibling",
    )(place, mine, other, weights, inverse, first)


def q_kernel(place_ref, mine_ref, other_ref, weight_ref, first_ref, out_ref):
    heads = by_core(place_ref[0])
    weights = jnp.concatenate([weight_ref[head, :, :QW] for head in heads], axis=0)
    out_ref[...] = contract(OWN, mine_ref, other_ref, weights)


def project_q(place, mine, other, weights, first):
    return pl.pallas_call(
        q_kernel,
        in_specs=[pl.BlockSpec(memory_space=pltpu.SMEM)]
        + [pl.BlockSpec(memory_space=pltpu.VMEM)] * 3
        + [pl.BlockSpec(memory_space=pl.ANY)],
        out_specs=pl.BlockSpec(memory_space=pltpu.VMEM),
        out_shape=jax.ShapeDtypeStruct((KMAX, QW), jnp.float32),
        compiler_params=params(),
        cost_estimate=pl.CostEstimate(flops=2**29, bytes_accessed=2**22, transcendentals=0),
        name="project_q",
    )(place, mine, other, weights, first)


def upper_kernel(place_ref, q_ref, kv_ref, square_ref, got_q_ref, got_last_ref, got_kv_ref, out_ref):
    parity = place_ref[1]
    own_count = place_ref[2]
    left_count = place_ref[3]
    tail = got_last_ref[KMAX:].astype(jnp.float32)
    same = lax.broadcasted_iota(jnp.int32, (KMAX, KMAX), 0) == lax.broadcasted_iota(
        jnp.int32, (KMAX, KMAX), 1
    )

    def down(across):
        return jnp.sum(jnp.where(same, across, 0.0), axis=1, keepdims=True)

    own_sum = square_ref[:KMAX, :1] + down(tail[0:1] + tail[1:2])
    pair_sum = square_ref[KMAX:, :1] + down(tail[2:3] + tail[3:4])
    own_inv = lax.rsqrt(own_sum / D + 1e-05)
    pair_inv = lax.rsqrt(pair_sum / D + 1e-05)
    got = jnp.concatenate([got_q_ref[...], got_last_ref[:KMAX]], axis=1)
    queries = ((q_ref[...] + got.astype(jnp.float32)) * own_inv).astype(jnp.bfloat16)
    own = (kv_ref[:KMAX] + got_kv_ref[:, :KVW].astype(jnp.float32)) * own_inv
    own = own.astype(jnp.bfloat16)
    pair = (kv_ref[KMAX:] + got_kv_ref[:, KVW : 2 * KVW].astype(jnp.float32)) * pair_inv
    pair = pair.astype(jnp.bfloat16)
    keys = jnp.concatenate([pair[:, :HD], own[:, :HD]], axis=0)
    values = with_ones(jnp.concatenate([pair[:, HD:], own[:, HD:]], axis=0))
    row = lax.broadcasted_iota(jnp.int32, (KMAX, 2 * KMAX), 0)
    col = lax.broadcasted_iota(jnp.int32, (KMAX, 2 * KMAX), 1)
    from_left = col < left_count * parity
    from_own = (col >= KMAX) & (col - KMAX <= row) & (col - KMAX < own_count)
    allowed = from_left | from_own
    valid = lax.broadcasted_iota(jnp.int32, (KMAX, HD), 0) < own_count
    for g in range(GROUP):
        cols = slice(g * HD, (g + 1) * HD)
        scores = jnp.where(allowed, dot_t(queries[:, cols], keys) * SCALE, NEG)
        out_ref[:, cols] = jnp.where(valid, attend(scores, values), 0.0).astype(jnp.bfloat16)


def upper(place, q, kv, squares, got_q, got_last, got_kv):
    return pl.pallas_call(
        upper_kernel,
        in_specs=[pl.BlockSpec(memory_space=pltpu.SMEM)] + [pl.BlockSpec(memory_space=pltpu.VMEM)] * 6,
        out_shape=jax.ShapeDtypeStruct((KMAX, QW), jnp.bfloat16),
        compiler_params=params(),
        name="upper",
    )(place, q, kv, squares, got_q, got_last, got_kv)


def gather_head(x):
    mine = lax.all_to_all(x, "head", 0, 0, axis_index_groups=X_GROUPS, tiled=True)
    return mine, lax.ppermute(mine, "head", CORE_SWAP)


def per_device(
    hidden,
    queries,
    keys_low,
    values_low,
    out_weight,
    norm_gain,
    query_weight,
    key_weight,
    value_weight,
    keep_index,
    keep_count,
):
    seq = lax.axis_index("seq")
    parity = seq % 2
    head = lax.axis_index("head")
    core = head % 2
    own_count = lax.dynamic_index_in_dim(keep_count, seq, keepdims=False)
    left_count = lax.dynamic_index_in_dim(keep_count, jnp.maximum(seq - 1, 0), keepdims=False)
    place = jnp.stack([core, parity, own_count, left_count, head]).astype(jnp.int32)

    shard = out_weight.T
    shards = lax.all_to_all(
        copies_of(shard),
        "seq",
        0,
        0,
        axis_index_groups=PARITY_GROUPS,
        tiled=True,
    )
    out_weights = lax.all_gather(
        shards.reshape(HALF, QW), "seq", axis=0, axis_index_groups=Z_GROUPS
    )

    gain = lax.dynamic_index_in_dim(
        norm_gain.reshape(8, N_Y // 2, 2, STRIP), parity, axis=2, keepdims=False
    ).reshape(8, 1, HALF)
    inverse = 1.0 / (gain * gain)
    index = keep_index.reshape(KMAX, 1)
    kept, hid = lower(place, index, queries, keys_low, values_low, hidden, gain, inverse)
    kept_pair = lax.ppermute(kept, "seq", SIBLING_SWAP)

    shard = jnp.concatenate([query_weight, key_weight, value_weight], axis=1)
    shards = lax.all_gather(shard, "seq", axis=0, axis_index_groups=PARITY_GROUPS, tiled=True)
    qkv_weights = lax.all_gather(shards, "seq", axis=0, axis_index_groups=Z_GROUPS)

    send = project(place, kept, kept_pair, out_weights, True)
    got = lax.ppermute(send, "head", CORE_SWAP)
    keep = project(place, kept, kept_pair, out_weights, False)
    parts = (keep + got.astype(jnp.float32)).astype(jnp.bfloat16)
    parts = lax.all_to_all(parts, "head", 0, 0, axis_index_groups=X_GROUPS, tiled=True)
    mine, other = gather_head(add_up(place, parts, hid, kept_pair, gain))

    kv, send = project_kv(place, mine, other, qkv_weights)
    got_kv = lax.ppermute(send, "seq", SIBLING_SWAP)
    squares, send, last = project_sibling(place, mine, other, qkv_weights, inverse, kv)
    got_q = lax.ppermute(send, "seq", SIBLING_SWAP)
    got_last = lax.ppermute(last, "seq", SIBLING_SWAP)
    q = project_q(place, mine, other, qkv_weights, send)
    return upper(place, q, kv, squares, got_q, got_last, got_kv)


def solution(mesh):
    in_specs = (
        P("seq", "head"),
        P("seq", "head"),
        P("seq", "head"),
        P("seq", "head"),
        P("head", "seq"),
        P(),
        P("seq", "head"),
        P("seq", "head"),
        P("seq", "head"),
        P("seq", None),
        P(),
    )
    out_specs = P("seq", "head")
    return jax.shard_map(
        per_device, mesh=mesh, in_specs=in_specs, out_specs=out_specs, check_vma=False
    )
```
